128 devices in a mesh: lat: 32 (over z, y_hi, x), lon: 4 (over y_lo, core).
Axes of the slice: x: 4, y: 4 (y_hi: 2, y_lo: 2; y = y_hi * 2 + y_lo), z: 4, core: 2. Of those that a mesh axis runs over, the one named last changes fastest.
Arguments:
- features: bfloat16 [192, 256, 768], P('lat', 'lon'), may hold values from -6 to 6
- upstream: bfloat16 [192, 256, 768], P('lat', 'lon'), may hold values from -6 to 6
- weights: bfloat16 [3072, 768], replicated, may hold values from -0.109375 to 0.109375
- filter_basis: bfloat16 [4, 192, 7, 7], replicated, may hold values from -0.875 to 0.875
- lat_width: int32 [192], replicated, may hold values from 1 to 7
- lat_offset: int32 [192], replicated, may hold values from 0 to 6, as said below
- lon_reach: int32 [192], replicated, may hold values from 0 to 3
Outputs:
- convolved: bfloat16 [192, 256, 768], P('lat', 'lon')
- state_grad: bfloat16 [192, 256, 768], P('lat', 'lon')
- weight_grad: float32 [3072, 768], P(('lat', 'lon'))
The draws below stay inside these ranges and needn't reach their ends.
Inputs may be any that keep to these rules, and one draw needn't show every extreme that they name: lat_offset + lat_width <= 7 at every latitude.
All inputs are finite; a program needn't handle non-finite values.
Results may differ from the reference program's by a relative error of at most 0.0055.
Values may be sent and summed in bfloat16 or wider, within the bound.
No kernel may reach another device: no remote copies, remote signals or barrier semaphores. Data moves between devices by JAX's collectives and lax.ppermute only.
A program may use at most 128 MiB of HBM per device.

```python
import jax
import jax.numpy as jnp
from jax import lax

CHANNELS = 768
NBASIS = 4
HALO = 3
TAPS = 7
NLAT = 192
NLON = 256


def support_draw(key):
    first_key, second_key = jax.random.split(key)
    row_ids = jnp.arange(NLAT, dtype=jnp.int32)
    width = jax.random.randint(first_key, (NLAT,), 1, TAPS + 1)
    width = jnp.where((row_ids == 0) | (row_ids == NLAT - 1), TAPS, width)
    width = jnp.where(row_ids == 1, 1, width)
    picks = jax.random.randint(second_key, (NLAT,), 0, TAPS)
    offset = picks % (TAPS - width + 1)
    offset = jnp.where(row_ids == 1, TAPS - 1, offset)
    return (width.astype(jnp.int32), offset.astype(jnp.int32))


def draw_lat_width(key, part):
    width, offset = support_draw(key)
    return width


def draw_lat_offset(key, part):
    width, offset = support_draw(key)
    return offset


def draw_lon_reach(key, part):
    key = jax.random.fold_in(key, 7)
    row_ids = jnp.arange(NLAT, dtype=jnp.int32)
    reach = jax.random.randint(key, (NLAT,), 0, HALO + 1)
    reach = jnp.where(row_ids == 0, HALO, reach)
    reach = jnp.where(row_ids == 1, 0, reach)
    return reach.astype(jnp.int32)


def block_scale(own_key, dims, cuts, low, largest):
    factor_of = 1.0
    for axis_at, blocks in cuts:
        steps = jax.random.uniform(jax.random.fold_in(jax.random.fold_in(own_key, 6), axis_at), (blocks,), jnp.float32, low / len(cuts), largest / len(cuts))
        factor_of = factor_of * jnp.repeat(jnp.exp(steps), dims[axis_at] // blocks).reshape((-1,) + (1,) * (len(dims) - 1 - axis_at))
    return factor_of


def gaussian(key, shape, deviation, limit, cuts=(), kind=jnp.bfloat16):
    array = jax.random.normal(key, shape, jnp.float32) * deviation
    if len(cuts) > 0:
        array = block_scale(key, shape, cuts, -0.22, 0.18) * array
    return jnp.clip(array, min=-limit, max=limit).astype(kind)


def setup_inputs(seed: int = 0) -> dict:
    seeds = jax.random.split(jax.random.key(seed), 8)
    features = gaussian(seeds[0], (NLAT, NLON, CHANNELS), 1.0, 6.0, ((0, 32), (1, 4)))
    upstream = gaussian(seeds[1], (NLAT, NLON, CHANNELS), 1.0, 6.0, ((0, 32), (1, 4)))
    weights = gaussian(seeds[2], (NBASIS * CHANNELS, CHANNELS), (NBASIS * CHANNELS) ** -0.5, 0.109375)
    filter_basis = gaussian(seeds[3], (NBASIS, NLAT, TAPS, TAPS), (TAPS * TAPS) ** -0.5, 0.875)
    lat_width = draw_lat_width(jax.random.fold_in(seeds[7], 71), 0)
    lat_offset = draw_lat_offset(jax.random.fold_in(seeds[7], 71), 0)
    lon_reach = draw_lon_reach(jax.random.fold_in(seeds[7], 71), 0)
    return dict(features=features, upstream=upstream, weights=weights, filter_basis=filter_basis, lat_width=lat_width, lat_offset=lat_offset, lon_reach=lon_reach)


def support_filter(filter_rows, widths, offsets, reaches):
    tap_ids = jnp.arange(TAPS, dtype=jnp.int32)
    lat_keep = (tap_ids[None, :] >= offsets[:, None]) & (tap_ids[None, :] < offsets[:, None] + widths[:, None])
    lon_keep = jnp.abs(tap_ids - HALO)[None, :] <= reaches[:, None]
    kept_taps = lat_keep[None, :, :, None] & lon_keep[None, :, None, :]
    return jnp.where(kept_taps, filter_rows, jnp.zeros_like(filter_rows))


def extend(source):
    half_turn = NLON // 2
    upper_rows = jnp.roll(source[:HALO][::-1], half_turn, axis=1)
    lower_rows = jnp.roll(source[NLAT - HALO:][::-1], half_turn, axis=1)
    stacked = jnp.concatenate([upper_rows, source, lower_rows], 0)
    return jnp.concatenate([stacked[:, NLON - HALO:], stacked, stacked[:, :HALO]], 1)


def fold(spread):
    half_turn = NLON // 2
    lon_folded = spread[:, HALO:HALO + NLON]
    lon_folded = lon_folded.at[:, :HALO].add(spread[:, HALO + NLON:])
    lon_folded = lon_folded.at[:, NLON - HALO:].add(spread[:, :HALO])
    lat_folded = lon_folded[HALO:HALO + NLAT]
    lat_folded = lat_folded.at[:HALO].add(jnp.roll(lon_folded[:HALO][::-1], half_turn, axis=1))
    lat_folded = lat_folded.at[NLAT - HALO:].add(jnp.roll(lon_folded[HALO + NLAT:][::-1], half_turn, axis=1))
    return lat_folded


def reference(features, upstream, weights, filter_basis, lat_width, lat_offset, lon_reach):
    filters = support_filter(filter_basis, lat_width, lat_offset, lon_reach).astype(jnp.float32)
    extended = extend(features)
    col_span = NLON + 2 * HALO
    zero_index = jnp.int32(0)

    def per_row(state_pair, inputs):
        grad_sum, spread = state_pair
        row_index, cot_row = inputs
        window = lax.dynamic_slice(extended, (row_index, zero_index, zero_index), (TAPS, col_span, CHANNELS)).astype(jnp.float32)
        row_taps = lax.dynamic_index_in_dim(filters, row_index, 1, keepdims=False)
        basis_row = jnp.zeros((NBASIS, NLON, CHANNELS), jnp.float32)
        for shift_col in range(TAPS):
            basis_row = basis_row + jnp.einsum("ka,ajc->kjc", row_taps[:, :, shift_col], window[:, shift_col:shift_col + NLON])
        flat_basis = jnp.transpose(basis_row.astype(jnp.bfloat16), (1, 0, 2)).reshape(NLON, NBASIS * CHANNELS)
        out_row = jnp.dot(flat_basis, weights, preferred_element_type=jnp.float32).astype(jnp.bfloat16)
        basis_grad = jnp.dot(cot_row, weights.T, preferred_element_type=jnp.float32).astype(jnp.bfloat16)
        basis_grad = lax.optimization_barrier(basis_grad)
        basis_grad = basis_grad.astype(jnp.float32).reshape(NLON, NBASIS, CHANNELS)
        grad_sum = grad_sum + jnp.dot(flat_basis.T, cot_row, preferred_element_type=jnp.float32)
        spread_rows = jnp.zeros((TAPS, col_span, CHANNELS), jnp.float32)
        for shift_col in range(TAPS):
            spread_rows = spread_rows.at[:, shift_col:shift_col + NLON].add(jnp.einsum("ka,jkc->ajc", row_taps[:, :, shift_col], basis_grad))
        previous = lax.dynamic_slice(spread, (row_index, zero_index, zero_index), (TAPS, col_span, CHANNELS))
        spread = lax.dynamic_update_slice(spread, previous + spread_rows, (row_index, zero_index, zero_index))
        return (grad_sum, spread), out_row

    start_pair = (jnp.zeros((NBASIS * CHANNELS, CHANNELS), jnp.float32), jnp.zeros((NLAT + 2 * HALO, col_span, CHANNELS), jnp.float32))
    (weight_grad, spread), convolved = lax.scan(per_row, start_pair, (jnp.arange(NLAT, dtype=jnp.int32), upstream))
    state_grad = fold(spread).astype(jnp.bfloat16)
    return convolved, state_grad, weight_grad
```

```python
import jax
import jax.numpy as jnp
from jax import lax
from jax.experimental import pallas as pl
from jax.experimental.pallas import tpu as pltpu
from jax.sharding import PartitionSpec as P

CHANNELS = 768
NBASIS = 4
HALO = 3
TAPS = 7
LAT = 32
LON = 4
ROWS = 6
COLS = 64
EDGE = 16
WIN = COLS + 2 * EDGE
EXT = ROWS + 2 * HALO
HALF = CHANNELS // 2
CELLS = ROWS * COLS
BAND = (TAPS + 1) * WIN
SPAN = NBASIS * WIN
BF = jnp.bfloat16
F32 = jnp.float32
BOTH = ("lat", "lon")

VMEM = pl.BlockSpec(memory_space=pltpu.VMEM)
SMEM = pl.BlockSpec(memory_space=pltpu.SMEM)
PARAMS = pltpu.CompilerParams(vmem_limit_bytes=56 * 1024 * 1024)


def route(move):
    pairs = []
    for lat in range(LAT):
        for lon in range(LON):
            to = move(lat, lon)
            if to is not None:
                pairs.append((lat * LON + lon, to[0] * LON + to[1]))
    return pairs


def send(block, move):
    return lax.ppermute(block, BOTH, route(move))


def to_partner(lat, lon):
    return lat, lon ^ 1


def to_chip(lat, lon):
    return lat, lon ^ 2


def down(lat, lon):
    return (lat + 1, lon) if lat + 1 < LAT else None


def up(lat, lon):
    return (lat - 1, lon) if lat > 0 else None


def down_chip(lat, lon):
    return (lat + 1, lon ^ 2) if lat + 1 < LAT else None


def up_chip(lat, lon):
    return (lat - 1, lon ^ 2) if lat > 0 else None


def mirror(lat, lon):
    return (lat, lon ^ 2) if lat in (0, LAT - 1) else None


def bands_kernel(vec_ref, band_ref):
    for i in range(ROWS):
        for k in range(NBASIS):
            row = jnp.broadcast_to(vec_ref[i, k : k + 1, :], (COLS, BAND))
            block = pltpu.roll(row, 0, 1, stride=1, stride_axis=0)
            band_ref[i, k * COLS : (k + 1) * COLS, :] = block.astype(BF)


def pack_kernel(flag, up_ref, down_ref, mirror_ref, edge_ref, up_edge_ref, down_edge_ref, own_edge_ref, out_ref):
    out_ref[:, COLS + EDGE :, :] = edge_ref[...]
    first = flag[1] == 1
    last = flag[2] == 1

    @pl.when(first)
    def _():
        for m in range(HALO):
            out_ref[m, :COLS, :] = mirror_ref[HALO - 1 - m]
            out_ref[m, COLS : COLS + EDGE, :] = own_edge_ref[HALO - 1 - m]

    @pl.when(jnp.logical_not(first))
    def _():
        for m in range(HALO):
            out_ref[m, :COLS, :] = up_ref[m]
            out_ref[m, COLS : COLS + EDGE, :] = up_edge_ref[m]

    @pl.when(last)
    def _():
        for m in range(HALO):
            out_ref[HALO + m, :COLS, :] = mirror_ref[HALO - 1 - m]
            out_ref[HALO + m, COLS : COLS + EDGE, :] = own_edge_ref[ROWS - 1 - m]

    @pl.when(jnp.logical_not(last))
    def _():
        for m in range(HALO):
            out_ref[HALO + m, :COLS, :] = down_ref[m]
            out_ref[HALO + m, COLS : COLS + EDGE, :] = down_edge_ref[m]


def fill_left(x, f0, h0, f1, h1):
    mid = slice(HALO, HALO + ROWS)
    x[mid, :EDGE, :] = h1[:, COLS + EDGE :, :]
    x[mid, EDGE : EDGE + COLS, :] = f0[...]
    x[mid, EDGE + COLS :, :] = f1[:, :EDGE, :]
    for at, src in ((slice(0, HALO), slice(0, HALO)), (slice(HALO + ROWS, EXT), slice(HALO, 2 * HALO))):
        x[at, :EDGE, :] = h1[src, COLS : COLS + EDGE, :]
        x[at, EDGE : EDGE + COLS, :] = h0[src, :COLS, :]
        x[at, EDGE + COLS :, :] = h1[src, :EDGE, :]


def fill_right(x, f0, h0, f1, h1):
    mid = slice(HALO, HALO + ROWS)
    x[mid, :EDGE, :] = f0[:, COLS - EDGE :, :]
    x[mid, EDGE : EDGE + COLS, :] = f1[...]
    x[mid, EDGE + COLS :, :] = h0[:, COLS + EDGE :, :]
    for at, src in ((slice(0, HALO), slice(0, HALO)), (slice(HALO + ROWS, EXT), slice(HALO, 2 * HALO))):
        x[at, :EDGE, :] = h0[src, COLS - EDGE : COLS, :]
        x[at, EDGE : EDGE + COLS, :] = h1[src, :COLS, :]
        x[at, EDGE + COLS :, :] = h0[src, COLS : COLS + EDGE, :]


def grad_kernel(flag, f_own, f_part, h_own, h_part, u_own, u_part, band_ref, g_ref, own_ref, x0, x1, basis, ud):
    core = flag[0]
    for x in (x0, x1):
        x[EXT : EXT + 1, :, :] = jnp.zeros((1, WIN, CHANNELS), BF)

    @pl.when(core == 0)
    def _():
        fill_left(x0, f_own, h_own, f_part, h_part)
        fill_right(x1, f_own, h_own, f_part, h_part)
        ud[:CELLS, :] = u_own[:, :, :HALF].reshape(CELLS, HALF)
        ud[CELLS:, :] = u_part[:, :, :HALF].reshape(CELLS, HALF)

    @pl.when(core == 1)
    def _():
        fill_left(x0, f_part, h_part, f_own, h_own)
        fill_right(x1, f_part, h_part, f_own, h_own)
        ud[:CELLS, :] = u_part[:, :, HALF:].reshape(CELLS, HALF)
        ud[CELLS:, :] = u_own[:, :, HALF:].reshape(CELLS, HALF)

    for i in range(ROWS):
        for w, x in enumerate((x0, x1)):
            cells = x[i : i + TAPS + 1].reshape(BAND, CHANNELS)
            rows = jnp.dot(band_ref[i], cells, preferred_element_type=F32).astype(BF)
            for k in range(NBASIS):
                basis[k, w * CELLS + i * COLS : w * CELLS + (i + 1) * COLS, :] = rows[k * COLS : (k + 1) * COLS]
    for k in range(NBASIS):
        g = lax.dot_general(basis[k], ud[...], (((0,), (0,)), ((), ())), preferred_element_type=F32)
        g_ref[k * CHANNELS : (k + 1) * CHANNELS, :] = g.astype(BF)

    @pl.when(core == 0)
    def _():
        own_ref[...] = basis[:, :CELLS, :]

    @pl.when(core == 1)
    def _():
        own_ref[...] = basis[:, CELLS:, :]


def local_kernel(flag, own_ref, w_ref, vec_ref, u_own, u_part, h_own, h_part, conv_ref, state_ref, x, bg, acc):
    core = flag[0]

    @pl.when(core == 0)
    def _():
        fill_left(x, u_own, h_own, u_part, h_part)

    @pl.when(core == 1)
    def _():
        fill_right(x, u_part, h_part, u_own, h_own)

    total = jnp.zeros((CELLS, CHANNELS), F32)
    for k in range(NBASIS):
        total = total + jnp.dot(own_ref[k], w_ref[k * CHANNELS : (k + 1) * CHANNELS, :], preferred_element_type=F32)
    conv_ref[...] = total.astype(BF).reshape(ROWS, COLS, CHANNELS)
    for k in range(NBASIS):
        wk = w_ref[k * CHANNELS : (k + 1) * CHANNELS, :]
        for part in range(3):
            cells = x[part * 4 : (part + 1) * 4].reshape(4 * WIN, CHANNELS)
            got = lax.dot_general(cells, wk, (((1,), (1,)), ((), ())), preferred_element_type=F32)
            bg[part * 4 : (part + 1) * 4, k * WIN : (k + 1) * WIN, :] = got.astype(BF).reshape(4, WIN, CHANNELS)
    acc[...] = jnp.zeros((ROWS, COLS, CHANNELS), F32)
    for e in range(EXT):
        rows = [r for r in range(ROWS) if 0 <= r + TAPS - 1 - e < TAPS]
        blocks = []
        for r in rows:
            a = r + TAPS - 1 - e
            row = jnp.broadcast_to(vec_ref[e, a : a + 1, :], (COLS, SPAN))
            blocks.append(pltpu.roll(row, 0, 1, stride=1, stride_axis=0).astype(BF))
        got = jnp.dot(jnp.concatenate(blocks, 0), bg[e], preferred_element_type=F32)
        for n, r in enumerate(rows):
            acc[r] += got[n * COLS : (n + 1) * COLS]
    state_ref[...] = acc[...].astype(BF)


def support_filter(filter_rows, widths, offsets, reaches):
    tap_ids = jnp.arange(TAPS, dtype=jnp.int32)
    lat_keep = (tap_ids[None, :] >= offsets[:, None]) & (
        tap_ids[None, :] < offsets[:, None] + widths[:, None]
    )
    lon_keep = jnp.abs(tap_ids - HALO)[None, :] <= reaches[:, None]
    kept_taps = lat_keep[None, :, :, None] & lon_keep[None, :, None, :]
    return jnp.where(kept_taps, filter_rows, jnp.zeros_like(filter_rows))


def extended_filters(filter_basis, lat_width, lat_offset, lon_reach, lat):
    start = lat * ROWS

    def rows(at, size):
        return support_filter(
            lax.dynamic_slice_in_dim(filter_basis, at, size, 1),
            lax.dynamic_slice_in_dim(lat_width, at, size, 0),
            lax.dynamic_slice_in_dim(lat_offset, at, size, 0),
            lax.dynamic_slice_in_dim(lon_reach, at, size, 0),
        )

    above = rows(jnp.maximum(start - HALO, 0), HALO)
    below = rows(jnp.minimum(start + ROWS, LAT * ROWS - HALO), HALO)
    above = jnp.where(lat == 0, above[:, ::-1, ::-1], above)
    below = jnp.where(lat == LAT - 1, below[:, ::-1, ::-1], below)
    return jnp.concatenate([above, rows(start, ROWS), below], 1)


def halo(field, core, lat, flag):
    edge = jnp.where(core == 0, field[:, :EDGE], field[:, COLS - EDGE :])
    head, tail = field[:HALO], field[ROWS - HALO :]
    from_up = send(tail, down)
    from_down = send(head, up)
    mirrored = send(jnp.where(lat == 0, head, tail), mirror)
    from_chip = send(edge, to_chip)
    up_edge = send(edge[ROWS - HALO :], down_chip)
    down_edge = send(edge[:HALO], up_chip)
    return pl.pallas_call(
        pack_kernel,
        out_shape=jax.ShapeDtypeStruct((ROWS, WIN, CHANNELS), BF),
        in_specs=[SMEM] + [VMEM] * 7,
        out_specs=VMEM,
        compiler_params=PARAMS,
        name="pack",
    )(flag, from_up, from_down, mirrored, from_chip, up_edge, down_edge, edge)


def on_device(features, upstream, weights, filter_basis, lat_width, lat_offset, lon_reach):
    lat = lax.axis_index("lat")
    core = lax.axis_index("lon") % 2
    flag = jnp.stack([core, lat == 0, lat == LAT - 1]).astype(jnp.int32)

    f_part = send(features, to_partner)
    u_part = send(upstream, to_partner)
    h_own = halo(features, core, lat, flag)
    h_part = send(h_own, to_partner)

    filters = extended_filters(filter_basis, lat_width, lat_offset, lon_reach, lat).astype(F32)
    own_rows = jnp.transpose(filters[:, HALO : HALO + ROWS], (1, 0, 2, 3))
    at = EDGE - HALO
    band_vec = jnp.pad(own_rows, ((0, 0), (0, 0), (0, 1), (at, WIN - at - TAPS))).reshape(ROWS, NBASIS, BAND)
    spread_rows = jnp.transpose(filters[:, :, :, ::-1], (1, 2, 0, 3))
    spread_vec = jnp.pad(spread_rows, ((0, 0), (0, 0), (0, 0), (at, WIN - at - TAPS))).reshape(EXT, TAPS, SPAN)
    bands = pl.pallas_call(
        bands_kernel,
        out_shape=jax.ShapeDtypeStruct((ROWS, NBASIS * COLS, BAND), BF),
        in_specs=[VMEM],
        out_specs=VMEM,
        compiler_params=PARAMS,
        name="bands",
    )(band_vec)

    partial, basis_own = pl.pallas_call(
        grad_kernel,
        out_shape=(
            jax.ShapeDtypeStruct((NBASIS * CHANNELS, HALF), BF),
            jax.ShapeDtypeStruct((NBASIS, CELLS, CHANNELS), BF),
        ),
        in_specs=[SMEM] + [VMEM] * 7,
        out_specs=(VMEM, VMEM),
        scratch_shapes=[
            pltpu.VMEM((EXT + 1, WIN, CHANNELS), BF),
            pltpu.VMEM((EXT + 1, WIN, CHANNELS), BF),
            pltpu.VMEM((NBASIS, 2 * CELLS, CHANNELS), BF),
            pltpu.VMEM((2 * CELLS, HALF), BF),
        ],
        compiler_params=PARAMS,
        cost_estimate=pl.CostEstimate(flops=5_400_000_000, bytes_accessed=12_000_000, transcendentals=0),
        name="grad",
    )(flag, features, f_part, h_own, h_part, upstream, u_part, bands)

    pieces = lax.all_to_all(partial.reshape(LAT * LON, 24, HALF), BOTH, 0, 0, tiled=True)

    hu_own = halo(upstream, core, lat, flag)
    hu_part = send(hu_own, to_partner)
    convolved, state_grad = pl.pallas_call(
        local_kernel,
        out_shape=(
            jax.ShapeDtypeStruct((ROWS, COLS, CHANNELS), BF),
            jax.ShapeDtypeStruct((ROWS, COLS, CHANNELS), BF),
        ),
        in_specs=[SMEM] + [VMEM] * 7,
        out_specs=(VMEM, VMEM),
        scratch_shapes=[
            pltpu.VMEM((EXT, WIN, CHANNELS), BF),
            pltpu.VMEM((EXT, SPAN, CHANNELS), BF),
            pltpu.VMEM((ROWS, COLS, CHANNELS), F32),
        ],
        compiler_params=PARAMS,
        cost_estimate=pl.CostEstimate(flops=9_000_000_000, bytes_accessed=12_000_000, transcendentals=0),
        name="local",
    )(flag, basis_own, weights, spread_vec, upstream, u_part, hu_own, hu_part)

    summed = pieces.astype(F32).reshape(LAT * LON // 2, 2, 24, HALF).sum(0)
    weight_grad = jnp.concatenate([summed[0], summed[1]], 1)
    return convolved, state_grad, weight_grad


def solution(mesh):
    return jax.shard_map(
        on_device,
        mesh=mesh,
        in_specs=(P("lat", "lon", None), P("lat", "lon", None), P(), P(), P(), P(), P()),
        out_specs=(P("lat", "lon", None), P("lat", "lon", None), P(("lat", "lon"), None)),
        check_vma=False,
    )
```

```python
import jax
import jax.numpy as jnp
from jax import lax
from jax.experimental import pallas as pl
from jax.experimental.pallas import tpu as pltpu
from jax.sharding import PartitionSpec as P

CHANNELS = 768
NBASIS = 4
HALO = 3
TAPS = 7
LAT = 32
LON = 4
NLAT = 192
ROWS = 6
COLS = 64
EDGE = 16
WIN = COLS + 2 * EDGE
CHIP = 2 * COLS
WIDE = CHIP + 2 * EDGE
EXT = ROWS + 2 * HALO
HALF = CHANNELS // 2
CELLS = ROWS * COLS
BAND = (TAPS + 1) * WIN
SPAN = NBASIS * WIN
PLACES = TAPS * TAPS * NBASIS
OWNED = NBASIS * CHANNELS // (LAT * LON)
BF = jnp.bfloat16
F32 = jnp.float32
BOTH = ("lat", "lon")
DEVICES = [(lat, lon) for lat in range(LAT) for lon in range(LON)]

VMEM = pl.BlockSpec(memory_space=pltpu.VMEM)
SMEM = pl.BlockSpec(memory_space=pltpu.SMEM)
ANY = pl.BlockSpec(memory_space=pl.ANY)
HBM = pl.BlockSpec(memory_space=pltpu.HBM)
MIB = 1024 * 1024


def params(mib):
    return pltpu.CompilerParams(vmem_limit_bytes=mib * MIB)


def cost(flops, size):
    return pl.CostEstimate(flops=flops, bytes_accessed=size, transcendentals=0)


def send(block, move):
    pairs = []
    for lat, lon in DEVICES:
        to = move(lat, lon)
        if to is not None:
            pairs.append((lat * LON + lon, to[0] * LON + to[1]))
    return lax.ppermute(block, BOTH, pairs)


def to_partner(lat, lon):
    return lat, lon ^ 1


def to_chip(lat, lon):
    return lat, lon ^ 2


def along_meridian(lat, lon):
    if lon % 2 == 0:
        return (lat + 1, lon) if lat + 1 < LAT else (lat, lon ^ 3)
    return (lat - 1, lon) if lat > 0 else (lat, lon ^ 3)


def across(lat, lon):
    to_lat = lat + 1 if lon % 2 == 0 else lat - 1
    return (to_lat, lon ^ 2) if 0 <= to_lat < LAT else None


def split(values, size):
    high = jnp.floor((values.astype(F32) + 0.5) * (1.0 / size)).astype(jnp.int32)
    return high, values - high * size


def bands_kernel(info, filt, band_ref, vec_ref):
    lat = info[1]
    lane = lax.broadcasted_iota(jnp.int32, (1, 128), 1)
    row_of = lat * ROWS + lane - HALO
    row_of = jnp.where(row_of < 0, -1 - row_of, row_of)
    row_of = jnp.where(row_of >= NLAT, 2 * NLAT - 1 - row_of, row_of)
    pick = lax.broadcasted_iota(jnp.int32, (NLAT, 128), 0) == row_of
    rows = jnp.dot(filt[...], pick.astype(F32).astype(BF), preferred_element_type=F32)
    low = jnp.zeros((1, 128), jnp.int32)
    high = jnp.zeros((1, 128), jnp.int32)
    far = jnp.zeros((1, 128), jnp.int32)
    for e in range(EXT):
        row = lat * ROWS + e - HALO
        row = jnp.where(row < 0, -1 - row, row)
        row = jnp.where(row >= NLAT, 2 * NLAT - 1 - row, row)
        width, offset, reach = info[2 + row], info[2 + NLAT + row], info[2 + 2 * NLAT + row]
        low = jnp.where(lane == e, offset, low)
        high = jnp.where(lane == e, offset + width, high)
        far = jnp.where(lane == e, reach, far)
    a, rest = split(lax.broadcasted_iota(jnp.int32, (PLACES, 128), 0), TAPS * NBASIS)
    b, _ = split(rest, NBASIS)
    keep = (a >= low) & (a < high) & (jnp.abs(b - HALO) <= far)
    rows = jnp.where(keep, rows, 0.0).astype(BF)
    over = (((0,), (0,)), ((), ()))
    a, b = split(lax.broadcasted_iota(jnp.int32, (1, BAND), 1), WIN)
    b = b - (EDGE - HALO)
    band_at = jnp.where((a < TAPS) & (b >= 0) & (b < TAPS), (a * TAPS + b) * NBASIS, -PLACES)
    place = lax.broadcasted_iota(jnp.int32, (PLACES, BAND), 0)
    for k in range(NBASIS):
        put = (place == band_at + k).astype(F32).astype(BF)
        vec = lax.dot_general(rows, put, over, preferred_element_type=F32)
        for i in range(ROWS):
            row = jnp.broadcast_to(vec[HALO + i : HALO + i + 1, :], (COLS, BAND))
            block = pltpu.roll(row, 0, 1, stride=1, stride_axis=0)
            band_ref[i, k * COLS : (k + 1) * COLS, :] = block.astype(BF)
    k, b = split(lax.broadcasted_iota(jnp.int32, (1, SPAN), 1), WIN)
    b = EDGE + HALO - b
    spread_at = jnp.where((b >= 0) & (b < TAPS), b * NBASIS + k, -PLACES)
    place = lax.broadcasted_iota(jnp.int32, (PLACES, SPAN), 0)
    vecs = []
    for a in range(TAPS):
        put = (place == spread_at + a * TAPS * NBASIS).astype(F32).astype(BF)
        vecs.append(lax.dot_general(rows, put, over, preferred_element_type=F32)[:16])
    e = lax.broadcasted_iota(jnp.int32, (16, SPAN), 0)
    beyond = ((lat == 0) & (e < HALO)) | ((lat == LAT - 1) & (e >= HALO + ROWS))
    for a in range(TAPS):
        vec_ref[a] = jnp.where(beyond, vecs[TAPS - 1 - a], vecs[a])


def each(todo, act):
    for c in todo:
        act(c)


def start_copy(c):
    c.start()


def wait_copy(c):
    c.wait()


def run(todo):
    each(todo, start_copy)
    each(todo, wait_copy)


def rows_kernel(info, own, part, out, sems):
    for core_is, row in enumerate((ROWS - HALO, 0)):
        low, high = slice(0, COLS), slice(COLS, CHIP)
        mine, other = (low, high) if core_is == 0 else (high, low)

        @pl.when(info[0] == core_is)
        def _():
            run(
                [
                    pltpu.make_async_copy(own, out.at[:, mine], sems.at[0]),
                    pltpu.make_async_copy(part.at[row : row + HALO], out.at[:, other], sems.at[1]),
                ]
            )


def relay_kernel(info, a_own, e_own, c_own, u_own, u_part, out, u_rows, sems):
    todo = [
        pltpu.make_async_copy(a_own, out.at[0:HALO], sems.at[0]),
        pltpu.make_async_copy(e_own, out.at[HALO, 0:COLS], sems.at[1]),
        pltpu.make_async_copy(c_own, out.at[HALO, COLS:CHIP], sems.at[2]),
    ]
    each(todo, start_copy)
    for core_is, row in enumerate((ROWS - HALO, 0)):
        half0, half1 = (u_own, u_part) if core_is == 0 else (u_part, u_own)
        at = slice(row, row + HALO)

        @pl.when(info[0] == core_is)
        def _():
            run(
                [
                    pltpu.make_async_copy(half0.at[at], u_rows.at[:, 0:COLS], sems.at[3]),
                    pltpu.make_async_copy(half1.at[at], u_rows.at[:, COLS:CHIP], sems.at[4]),
                ]
            )

    each(todo, wait_copy)


def slots(which, group):
    at = (2 * which + group) * EDGE
    return slice(at, at + EDGE)


def gather_columns(rows, first):
    slot = lax.broadcasted_iota(jnp.int32, (EDGE, CHANNELS), 0)
    out = jnp.zeros((EDGE, CHANNELS), F32)
    for m, row in enumerate(rows):
        shift = (4 * m - (0 if first else EDGE - HALO)) % EDGE
        moved = pltpu.roll(row.astype(F32), shift, 0)
        out = jnp.where((slot >= 4 * m) & (slot < 4 * m + HALO), moved, out)
    return out.astype(BF)


def spread_columns(block, m, first):
    slot = lax.broadcasted_iota(jnp.int32, (EDGE, CHANNELS), 0)
    moved = pltpu.roll(block.astype(F32), ((0 if first else EDGE - HALO) - 4 * m) % EDGE, 0)
    keep = slot < HALO if first else slot >= EDGE - HALO
    return jnp.where(keep, moved, 0.0).astype(BF)


def edges_kernel(info, f_own, f_part, u_own, u_part, after, edge, corner, outer, sides, sems):
    first, last = slice(0, EDGE), slice(COLS - EDGE, COLS)

    def copies(columns, row, halves):
        todo = []
        for n, (own, half0, half1) in enumerate(halves):
            at = pl.ds(row, HALO)
            todo.append(pltpu.make_async_copy(own.at[:, columns], outer.at[n], sems.at[3 * n]))
            todo.append(pltpu.make_async_copy(half0.at[at, first], sides.at[n, 0], sems.at[3 * n + 1]))
            todo.append(pltpu.make_async_copy(half1.at[at, last], sides.at[n, 1], sems.at[3 * n + 2]))
        return todo

    @pl.when(info[0] == 0)
    def _():
        run(copies(first, ROWS - HALO, ((f_own, f_own, f_part), (u_own, u_own, u_part))))
        for n in range(2):
            for g in range(2):
                edge[slots(n, g)] = gather_columns([outer[n, 3 * g + m] for m in range(HALO)], True)

    @pl.when(info[0] == 1)
    def _():
        run(copies(last, 0, ((f_own, f_part, f_own), (u_own, u_part, u_own))))
        for n in range(2):
            for g in range(2):
                edge[slots(n, g)] = gather_columns([outer[n, 3 * g + m] for m in range(HALO)], False)

    for n in range(2):
        for side in range(2):
            corner[slots(n, side)] = gather_columns([sides[n, side, m] for m in range(HALO)], side == 0)


def fill_copies(x, rim, sems, which, lat_is, half0, half1, passed0, passed1, rows0, rows1, start, stop):
    todo = []

    def put(ref, columns, at, rows, n):
        low, high = max(at, start), min(at + columns.stop - columns.start, stop)
        if low < high:
            src = ref.at[:, columns.start + low - at : columns.start + high - at]
            todo.append(pltpu.make_async_copy(src, x.at[rows, low - start : high - start], sems.at[n]))

    def put_row(ref, row, columns, at, to, n):
        low, high = max(at, start), min(at + columns.stop - columns.start, stop)
        if low < high:
            src = ref.at[row, columns.start + low - at : columns.start + high - at]
            todo.append(pltpu.make_async_copy(src, x.at[to, low - start : high - start], sems.at[n]))

    whole, first, last = slice(0, COLS), slice(0, EDGE), slice(COLS - EDGE, COLS)
    left, right = 0, EDGE + CHIP
    mid = slice(HALO, HALO + ROWS)
    for n, (ref, at) in enumerate(((passed1, 0), (passed0, 0), (passed0, COLS), (passed1, COLS))):
        at += 2 * EDGE * which
        todo.append(pltpu.make_async_copy(ref.at[HALO, at : at + 2 * EDGE], rim.at[n], sems.at[n]))
    put(half0, whole, EDGE, mid, 4)
    put(half1, whole, EDGE + COLS, mid, 5)
    n = 6
    for side, rows in enumerate((rows0, rows1)):
        to = side * (HALO + ROWS)
        if lat_is == side:
            for m in range(HALO):
                own = HALO - 1 - m + side * (ROWS - HALO)
                put_row(rows, HALO - 1 - m, slice(0, CHIP), EDGE, to + m, n + 3 * m)
                put_row(half1, own, last, left, to + m, n + 3 * m + 1)
                put_row(half0, own, first, right, to + m, n + 3 * m + 2)
        else:
            put(rows.at[0:HALO], slice(0, CHIP), EDGE, slice(to, to + HALO), n)
        n += 9
    return todo


FILL_SEMS = 24


def fill(act, info, x, rim, sems, which, half, passed, rows, window):
    core, lat = info[0], info[1]
    for core_is in range(2):
        refs = [pair[core_is ^ c] for pair in (half, passed, rows) for c in range(2)]
        start, stop = (core_is * COLS, core_is * COLS + WIN) if window else (0, WIDE)
        for lat_is, here in ((0, lat == 0), (1, lat == LAT - 1), (None, (lat > 0) & (lat < LAT - 1))):

            @pl.when((core == core_is) & here)
            def _():
                each(fill_copies(x, rim, sems, which, lat_is, *refs, start, stop), act)


def fill_rim(info, x, rim, left, right):
    lat = info[1]
    for at, first in ((left, False), (right, True)):
        if at is None:
            continue
        to = slice(at, at + EDGE)
        for r in range(ROWS):
            x[HALO + r, to, :] = spread_columns(rim[int(first), slots(0, r // HALO)], r % HALO, first)
        for side, pole in ((0, 0), (1, LAT - 1)):

            @pl.when(lat != pole)
            def _():
                for m in range(HALO):
                    x[side * (HALO + ROWS) + m, to, :] = spread_columns(rim[2 + side, slots(0, 1 - int(first))], m, first)


def grad_kernel(info, f_own, f_part, p_own, p_part, u_own, u_part, bands, g_ref, own_ref, x, rim, band, basis, ud, g, sems):
    core = info[0]
    band_copy = pltpu.make_async_copy(bands, band, sems.at[FILL_SEMS])

    def inputs(act):
        fill(act, info, x, rim, sems, 0, (f_own, f_part), (p_own, p_part), (p_own, p_part), False)
        for core_is, (u0, u1) in enumerate(((u_own, u_part), (u_part, u_own))):
            cols = slice(core_is * HALF, (core_is + 1) * HALF)

            @pl.when(core == core_is)
            def _():
                act(pltpu.make_async_copy(u0.at[:, :, cols], ud.at[0:ROWS], sems.at[FILL_SEMS + 1]))
                act(pltpu.make_async_copy(u1.at[:, :, cols], ud.at[ROWS : 2 * ROWS], sems.at[FILL_SEMS + 2]))

    inputs(start_copy)
    band_copy.start()
    x[EXT : EXT + 1, :, :] = jnp.zeros((1, WIDE, CHANNELS), BF)
    band_copy.wait()
    inputs(wait_copy)
    fill_rim(info, x, rim, 0, EDGE + CHIP)
    for i in range(ROWS):
        for w in range(2):
            cells = x[i : i + TAPS + 1, w * COLS : w * COLS + WIN].reshape(BAND, CHANNELS)
            rows = jnp.dot(band[i], cells, preferred_element_type=F32).astype(BF)
            for k in range(NBASIS):
                basis[k, w * CELLS + i * COLS : w * CELLS + (i + 1) * COLS, :] = rows[k * COLS : (k + 1) * COLS]
    at = pl.multiple_of(core * CELLS, CELLS)
    own_copy = pltpu.make_async_copy(basis.at[:, pl.ds(at, CELLS)], own_ref, sems.at[FILL_SEMS])
    own_copy.start()
    up = ud[...].reshape(2 * CELLS, HALF)
    outs = []
    for k in range(NBASIS):
        to = slice(k * CHANNELS, (k + 1) * CHANNELS)
        g[to, :] = lax.dot_general(basis[k], up, (((0,), (0,)), ((), ())), preferred_element_type=F32).astype(BF)
        outs.append(pltpu.make_async_copy(g.at[to], g_ref.at[to], sems.at[k]))
        outs[-1].start()
    own_copy.wait()
    each(outs, wait_copy)


def tie_kernel(partial, after, out):
    del partial, after, out


def local_kernel(info, own_ref, w_ref, vec_ref, u_own, u_part, p_own, p_part, a_own, a_part, conv_ref, state_ref, x, rim, bg, acc, sems):
    def inputs(act):
        fill(act, info, x, rim, sems, 1, (u_own, u_part), (p_own, p_part), (a_own, a_part), True)

    inputs(start_copy)
    total = jnp.zeros((CELLS, CHANNELS), F32)
    for k in range(NBASIS):
        total = total + jnp.dot(own_ref[k], w_ref[k * CHANNELS : (k + 1) * CHANNELS, :], preferred_element_type=F32)
    conv_ref[...] = total.astype(BF).reshape(ROWS, COLS, CHANNELS)
    inputs(wait_copy)

    @pl.when(info[0] == 0)
    def _():
        fill_rim(info, x, rim, 0, None)

    @pl.when(info[0] == 1)
    def _():
        fill_rim(info, x, rim, None, WIN - EDGE)

    for k in range(NBASIS):
        wk = w_ref[k * CHANNELS : (k + 1) * CHANNELS, :]
        for part in range(3):
            cells = x[part * 4 : (part + 1) * 4].reshape(4 * WIN, CHANNELS)
            got = lax.dot_general(cells, wk, (((1,), (1,)), ((), ())), preferred_element_type=F32)
            bg[part * 4 : (part + 1) * 4, k * WIN : (k + 1) * WIN, :] = got.astype(BF).reshape(4, WIN, CHANNELS)
    acc[...] = jnp.zeros((ROWS, COLS, CHANNELS), F32)
    for e in range(EXT):
        rows = [r for r in range(ROWS) if 0 <= r + TAPS - 1 - e < TAPS]
        blocks = []
        for r in rows:
            a = r + TAPS - 1 - e
            row = jnp.broadcast_to(vec_ref[a, e : e + 1, :], (COLS, SPAN))
            blocks.append(pltpu.roll(row, 0, 1, stride=1, stride_axis=0).astype(BF))
        got = jnp.dot(jnp.concatenate(blocks, 0), bg[e], preferred_element_type=F32)
        for n, r in enumerate(rows):
            acc[r] += got[n * COLS : (n + 1) * COLS]
    state_ref[...] = acc[...].astype(BF)


def on_device(features, upstream, weights, filter_basis, lat_width, lat_offset, lon_reach):
    lat = lax.axis_index("lat")
    core = lax.axis_index("lon") % 2
    info = jnp.concatenate([jnp.stack([core, lat]).astype(jnp.int32), lat_width, lat_offset, lon_reach])

    f_part = send(features, to_partner)
    u_part = send(upstream, to_partner)
    own_rows = jnp.where(core == 0, features[ROWS - HALO :], features[:HALO])
    rows = pl.pallas_call(
        rows_kernel,
        out_shape=jax.ShapeDtypeStruct((HALO, CHIP, CHANNELS), BF),
        in_specs=[SMEM, ANY, ANY],
        out_specs=ANY,
        scratch_shapes=[pltpu.SemaphoreType.DMA((2,))],
        compiler_params=params(4),
        cost_estimate=cost(1000, 2_000_000),
        name="rows",
    )(info, own_rows, f_part)
    af_own = send(rows, along_meridian)
    filt = jnp.transpose(filter_basis, (2, 3, 0, 1)).reshape(PLACES, NLAT)
    bands, vecs = pl.pallas_call(
        bands_kernel,
        out_shape=(
            jax.ShapeDtypeStruct((ROWS, NBASIS * COLS, BAND), BF),
            jax.ShapeDtypeStruct((TAPS, 16, SPAN), F32),
        ),
        in_specs=[SMEM, VMEM],
        out_specs=(VMEM, VMEM),
        compiler_params=params(16),
        cost_estimate=cost(2_000_000_000, 5_000_000),
        name="bands",
    )(info, filt)

    edges, corners = pl.pallas_call(
        edges_kernel,
        out_shape=(
            jax.ShapeDtypeStruct((COLS, CHANNELS), BF),
            jax.ShapeDtypeStruct((COLS, CHANNELS), BF),
        ),
        in_specs=[SMEM] + [ANY] * 5,
        out_specs=(VMEM, VMEM),
        scratch_shapes=[
            pltpu.VMEM((2, ROWS, EDGE, CHANNELS), BF),
            pltpu.VMEM((2, 2, HALO, EDGE, CHANNELS), BF),
            pltpu.SemaphoreType.DMA((6,)),
        ],
        compiler_params=params(4),
        cost_estimate=cost(1000, 1_000_000),
        name="edges",
    )(info, features, f_part, upstream, u_part, vecs)
    e_own = send(edges, to_chip)
    c_own = send(corners, across)
    passed, u_rows = pl.pallas_call(
        relay_kernel,
        out_shape=(
            jax.ShapeDtypeStruct((HALO + 1, CHIP, CHANNELS), BF),
            jax.ShapeDtypeStruct((HALO, CHIP, CHANNELS), BF),
        ),
        in_specs=[SMEM] + [ANY] * 5,
        out_specs=(ANY, ANY),
        scratch_shapes=[pltpu.SemaphoreType.DMA((5,))],
        compiler_params=params(4),
        cost_estimate=cost(1000, 4_000_000),
        name="relay",
    )(info, af_own, e_own, c_own, upstream, u_part)
    p_part = send(passed, to_partner)
    au_own = send(u_rows, along_meridian)
    au_part = send(au_own, to_partner)

    partial, basis_own = pl.pallas_call(
        grad_kernel,
        out_shape=(
            jax.ShapeDtypeStruct((NBASIS * CHANNELS, HALF), BF),
            pltpu.HBM((NBASIS, CELLS, CHANNELS), BF),
        ),
        in_specs=[SMEM] + [ANY] * 7,
        out_specs=(HBM, HBM),
        scratch_shapes=[
            pltpu.VMEM((EXT + 1, WIDE, CHANNELS), BF),
            pltpu.VMEM((4, 2 * EDGE, CHANNELS), BF),
            pltpu.VMEM((ROWS, NBASIS * COLS, BAND), BF),
            pltpu.VMEM((NBASIS, 2 * CELLS, CHANNELS), BF),
            pltpu.VMEM((2 * ROWS, COLS, HALF), BF),
            pltpu.VMEM((NBASIS * CHANNELS, HALF), BF),
            pltpu.SemaphoreType.DMA((FILL_SEMS + 3,)),
        ],
        compiler_params=params(32),
        cost_estimate=cost(8_000_000_000, 12_000_000),
        name="grad",
    )(info, features, f_part, passed, p_part, upstream, u_part, bands)

    partial = pl.pallas_call(
        tie_kernel,
        out_shape=jax.ShapeDtypeStruct(partial.shape, BF),
        in_specs=[ANY, ANY],
        out_specs=ANY,
        input_output_aliases={0: 0},
        compiler_params=params(1),
        name="tie",
    )(partial, au_own)
    pieces = lax.all_to_all(partial.reshape(LAT * LON, OWNED, HALF), BOTH, 0, 0, tiled=True)

    convolved, state_grad = pl.pallas_call(
        local_kernel,
        out_shape=(
            jax.ShapeDtypeStruct((ROWS, COLS, CHANNELS), BF),
            jax.ShapeDtypeStruct((ROWS, COLS, CHANNELS), BF),
        ),
        in_specs=[SMEM] + [VMEM] * 3 + [ANY] * 6,
        out_specs=(VMEM, VMEM),
        scratch_shapes=[
            pltpu.VMEM((EXT, WIN, CHANNELS), BF),
            pltpu.VMEM((4, 2 * EDGE, CHANNELS), BF),
            pltpu.VMEM((EXT, SPAN, CHANNELS), BF),
            pltpu.VMEM((ROWS, COLS, CHANNELS), F32),
            pltpu.SemaphoreType.DMA((FILL_SEMS,)),
        ],
        compiler_params=params(32),
        cost_estimate=cost(10_000_000_000, 12_000_000),
        name="local",
    )(info, basis_own, weights, vecs, upstream, u_part, passed, p_part, au_own, au_part)

    summed = pieces.astype(F32).reshape(LAT * LON // 2, 2, OWNED, HALF).sum(0)
    weight_grad = jnp.concatenate([summed[0], summed[1]], 1)
    return convolved, state_grad, weight_grad


def solution(mesh):
    return jax.shard_map(
        on_device,
        mesh=mesh,
        in_specs=(P("lat", "lon", None), P("lat", "lon", None), P(), P(), P(), P(), P()),
        out_specs=(P("lat", "lon", None), P("lat", "lon", None), P(("lat", "lon"), None)),
        check_vma=False,
    )
```

```python
import jax
import jax.numpy as jnp
from jax import lax
from jax.experimental import pallas as pl
from jax.experimental.pallas import tpu as pltpu
from jax.sharding import PartitionSpec as P

CHANNELS = 768
NBASIS = 4
HALO = 3
TAPS = 7
LAT = 32
LON = 4
NLAT = 192
ROWS = 6
COLS = 64
EDGE = 16
WIN = COLS + 2 * EDGE
CHIP = 2 * COLS
WIDE = CHIP + 2 * EDGE
EXT = ROWS + 2 * HALO
HALF = CHANNELS // 2
CELLS = ROWS * COLS
BAND = (TAPS + 1) * WIN
SPAN = NBASIS * WIN
PLACES = TAPS * TAPS * NBASIS
OWNED = NBASIS * CHANNELS // (LAT * LON)
BF = jnp.bfloat16
F32 = jnp.float32
BOTH = ("lat", "lon")
DEVICES = [(lat, lon) for lat in range(LAT) for lon in range(LON)]

VMEM = pl.BlockSpec(memory_space=pltpu.VMEM)
SMEM = pl.BlockSpec(memory_space=pltpu.SMEM)
ANY = pl.BlockSpec(memory_space=pl.ANY)
HBM = pl.BlockSpec(memory_space=pltpu.HBM)
MIB = 1024 * 1024


def params(mib):
    return pltpu.CompilerParams(vmem_limit_bytes=mib * MIB)


def in_hbm(block):
    return pltpu.with_memory_space_constraint(block, pltpu.HBM)


def cost(flops, size):
    return pl.CostEstimate(flops=flops, bytes_accessed=size, transcendentals=0)


def send(block, move):
    pairs = []
    for lat, lon in DEVICES:
        to = move(lat, lon)
        if to is not None:
            pairs.append((lat * LON + lon, to[0] * LON + to[1]))
    return lax.ppermute(block, BOTH, pairs)


def to_partner(lat, lon):
    return lat, lon ^ 1


def to_chip(lat, lon):
    return lat, lon ^ 2


def along_meridian(lat, lon):
    if lon % 2 == 0:
        return (lat + 1, lon) if lat + 1 < LAT else (lat, lon ^ 3)
    return (lat - 1, lon) if lat > 0 else (lat, lon ^ 3)


def across(lat, lon):
    to_lat = lat + 1 if lon % 2 == 0 else lat - 1
    return (to_lat, lon ^ 2) if 0 <= to_lat < LAT else None


def split(values, size):
    high = jnp.floor((values.astype(F32) + 0.5) * (1.0 / size)).astype(jnp.int32)
    return high, values - high * size


def bands_kernel(info, filt, band_ref, vec_ref):
    lat = my_lat()
    lane = lax.broadcasted_iota(jnp.int32, (1, 128), 1)
    row_of = lat * ROWS + lane - HALO
    row_of = jnp.where(row_of < 0, -1 - row_of, row_of)
    row_of = jnp.where(row_of >= NLAT, 2 * NLAT - 1 - row_of, row_of)
    pick = lax.broadcasted_iota(jnp.int32, (NLAT, 128), 0) == row_of
    rows = jnp.dot(filt[...], pick.astype(F32).astype(BF), preferred_element_type=F32)
    low = jnp.zeros((1, 128), jnp.int32)
    high = jnp.zeros((1, 128), jnp.int32)
    far = jnp.zeros((1, 128), jnp.int32)
    for e in range(EXT):
        row = lat * ROWS + e - HALO
        row = jnp.where(row < 0, -1 - row, row)
        row = jnp.where(row >= NLAT, 2 * NLAT - 1 - row, row)
        width, offset, reach = info[row], info[NLAT + row], info[2 * NLAT + row]
        low = jnp.where(lane == e, offset, low)
        high = jnp.where(lane == e, offset + width, high)
        far = jnp.where(lane == e, reach, far)
    a, rest = split(lax.broadcasted_iota(jnp.int32, (PLACES, 128), 0), TAPS * NBASIS)
    b, _ = split(rest, NBASIS)
    keep = (a >= low) & (a < high) & (jnp.abs(b - HALO) <= far)
    rows = jnp.where(keep, rows, 0.0).astype(BF)
    over = (((0,), (0,)), ((), ()))
    a, b = split(lax.broadcasted_iota(jnp.int32, (1, BAND), 1), WIN)
    b = b - (EDGE - HALO)
    band_at = jnp.where((a < TAPS) & (b >= 0) & (b < TAPS), (a * TAPS + b) * NBASIS, -PLACES)
    place = lax.broadcasted_iota(jnp.int32, (PLACES, BAND), 0)
    for k in range(NBASIS):
        put = (place == band_at + k).astype(F32).astype(BF)
        vec = lax.dot_general(rows, put, over, preferred_element_type=F32)
        for i in range(ROWS):
            row = jnp.broadcast_to(vec[HALO + i : HALO + i + 1, :], (COLS, BAND))
            block = pltpu.roll(row, 0, 1, stride=1, stride_axis=0)
            band_ref[i, k * COLS : (k + 1) * COLS, :] = block.astype(BF)
    k, b = split(lax.broadcasted_iota(jnp.int32, (1, SPAN), 1), WIN)
    b = EDGE + HALO - b
    spread_at = jnp.where((b >= 0) & (b < TAPS), b * NBASIS + k, -PLACES)
    place = lax.broadcasted_iota(jnp.int32, (PLACES, SPAN), 0)
    vecs = []
    for a in range(TAPS):
        put = (place == spread_at + a * TAPS * NBASIS).astype(F32).astype(BF)
        vecs.append(lax.dot_general(rows, put, over, preferred_element_type=F32)[:16])
    e = lax.broadcasted_iota(jnp.int32, (16, SPAN), 0)
    beyond = ((lat == 0) & (e < HALO)) | ((lat == LAT - 1) & (e >= HALO + ROWS))
    for a in range(TAPS):
        vec_ref[a] = jnp.where(beyond, vecs[TAPS - 1 - a], vecs[a])


def each(todo, act):
    for c in todo:
        act(c)


def start_copy(c):
    c.start()


def wait_copy(c):
    c.wait()


def my_core():
    return lax.rem(lax.axis_index("lon"), 2)


def my_lat():
    return lax.axis_index("lat")


def run(todo):
    each(todo, start_copy)
    each(todo, wait_copy)


def rows_kernel(own, part, out, sems):
    for core_is, row in enumerate((ROWS - HALO, 0)):
        low, high = slice(0, COLS), slice(COLS, CHIP)
        mine, other = (low, high) if core_is == 0 else (high, low)

        @pl.when(my_core() == core_is)
        def _():
            run(
                [
                    pltpu.make_async_copy(own, out.at[:, mine], sems.at[0]),
                    pltpu.make_async_copy(part.at[row : row + HALO], out.at[:, other], sems.at[1]),
                ]
            )


def relay_kernel(a_own, e_own, c_own, u_own, u_part, out, u_rows, sems):
    todo = [
        pltpu.make_async_copy(a_own, out.at[0:HALO], sems.at[0]),
        pltpu.make_async_copy(e_own, out.at[HALO, 0:PACKED], sems.at[1]),
        pltpu.make_async_copy(c_own, out.at[HALO, COLS : COLS + PACKED], sems.at[2]),
    ]
    each(todo, start_copy)
    for core_is, row in enumerate((ROWS - HALO, 0)):
        half0, half1 = (u_own, u_part) if core_is == 0 else (u_part, u_own)
        at = slice(row, row + HALO)

        @pl.when(my_core() == core_is)
        def _():
            run(
                [
                    pltpu.make_async_copy(half0.at[at], u_rows.at[:, 0:COLS], sems.at[3]),
                    pltpu.make_async_copy(half1.at[at], u_rows.at[:, COLS:CHIP], sems.at[4]),
                ]
            )

    each(todo, wait_copy)


PACKED = 3 * EDGE


def gather_columns(rows, firsts):
    slot = lax.broadcasted_iota(jnp.int32, (EDGE, CHANNELS), 0)
    out = jnp.zeros((EDGE, CHANNELS), F32)
    for m, (row, first) in enumerate(zip(rows, firsts)):
        shift = (4 * m - (0 if first else EDGE - HALO)) % EDGE
        moved = pltpu.roll(row.astype(F32), shift, 0)
        out = jnp.where((slot >= 4 * m) & (slot < 4 * m + HALO), moved, out)
    return out.astype(BF)


def pack_columns(out, rows, firsts):
    for g in range(3):
        four = slice(4 * g, 4 * g + 4)
        out[g * EDGE : (g + 1) * EDGE] = gather_columns(rows[four], firsts[four])


def spread_columns(rim, which, row, first):
    at = 2 * HALO * which + row
    block, m = at // 4 - which, at % 4
    slot = lax.broadcasted_iota(jnp.int32, (EDGE, CHANNELS), 0)
    shift = ((0 if first else EDGE - HALO) - 4 * m) % EDGE
    moved = pltpu.roll(rim[block * EDGE : (block + 1) * EDGE].astype(F32), shift, 0)
    keep = slot < HALO if first else slot >= EDGE - HALO
    return jnp.where(keep, moved, 0.0).astype(BF)


def edges_kernel(f_own, f_part, u_own, u_part, after, edge, corner, outer, sides, sems):
    first, last = slice(0, EDGE), slice(COLS - EDGE, COLS)

    def copies(columns, row, halves):
        todo = []
        for n, (own, half0, half1) in enumerate(halves):
            at = pl.ds(row, HALO)
            todo.append(pltpu.make_async_copy(own.at[:, columns], outer.at[n], sems.at[3 * n]))
            todo.append(pltpu.make_async_copy(half0.at[at, first], sides.at[n, 0], sems.at[3 * n + 1]))
            todo.append(pltpu.make_async_copy(half1.at[at, last], sides.at[n, 1], sems.at[3 * n + 2]))
        return todo

    @pl.when(my_core() == 0)
    def _():
        run(copies(first, ROWS - HALO, ((f_own, f_own, f_part), (u_own, u_own, u_part))))
        pack_columns(edge, [outer[n, r] for n in range(2) for r in range(ROWS)], [True] * (2 * ROWS))

    @pl.when(my_core() == 1)
    def _():
        run(copies(last, 0, ((f_own, f_part, f_own), (u_own, u_part, u_own))))
        pack_columns(edge, [outer[n, r] for n in range(2) for r in range(ROWS)], [False] * (2 * ROWS))

    places = [(n, side, m) for n in range(2) for side in range(2) for m in range(HALO)]
    pack_columns(corner, [sides[at] for at in places], [side == 0 for _, side, _ in places])


def fill_copies(x, rim, sems, which, lat_is, half0, half1, passed0, passed1, rows0, rows1, start, stop):
    todo = []

    def put(ref, columns, at, rows, n):
        low, high = max(at, start), min(at + columns.stop - columns.start, stop)
        if low < high:
            src = ref.at[:, columns.start + low - at : columns.start + high - at]
            todo.append(pltpu.make_async_copy(src, x.at[rows, low - start : high - start], sems.at[n]))

    def put_row(ref, row, columns, at, to, n):
        low, high = max(at, start), min(at + columns.stop - columns.start, stop)
        if low < high:
            src = ref.at[row, columns.start + low - at : columns.start + high - at]
            todo.append(pltpu.make_async_copy(src, x.at[to, low - start : high - start], sems.at[n]))

    whole, first, last = slice(0, COLS), slice(0, EDGE), slice(COLS - EDGE, COLS)
    left, right = 0, EDGE + CHIP
    mid = slice(HALO, HALO + ROWS)
    for n, (ref, at) in enumerate(((passed1, 0), (passed0, 0), (passed0, COLS), (passed1, COLS))):
        at += EDGE * which
        todo.append(pltpu.make_async_copy(ref.at[HALO, at : at + 2 * EDGE], rim.at[n], sems.at[n]))
    put(half0, whole, EDGE, mid, 4)
    put(half1, whole, EDGE + COLS, mid, 5)
    n = 6
    for side, rows in enumerate((rows0, rows1)):
        to = side * (HALO + ROWS)
        if lat_is == side:
            for m in range(HALO):
                own = HALO - 1 - m + side * (ROWS - HALO)
                put_row(rows, HALO - 1 - m, slice(0, CHIP), EDGE, to + m, n + 3 * m)
                put_row(half1, own, last, left, to + m, n + 3 * m + 1)
                put_row(half0, own, first, right, to + m, n + 3 * m + 2)
        else:
            put(rows.at[0:HALO], slice(0, CHIP), EDGE, slice(to, to + HALO), n)
        n += 9
    return todo


FILL_SEMS = 24


def fill(act, x, rim, sems, which, half, passed, rows, window):
    core, lat = my_core(), my_lat()
    for core_is in range(2):
        refs = [pair[core_is ^ c] for pair in (half, passed, rows) for c in range(2)]
        start, stop = (core_is * COLS, core_is * COLS + WIN) if window else (0, WIDE)
        for lat_is, here in ((0, lat == 0), (1, lat == LAT - 1), (None, (lat > 0) & (lat < LAT - 1))):

            @pl.when((core == core_is) & here)
            def _():
                each(fill_copies(x, rim, sems, which, lat_is, *refs, start, stop), act)


def fill_rim(x, rim, which, left, right):
    lat = my_lat()
    for at, first in ((left, False), (right, True)):
        if at is None:
            continue
        to = slice(at, at + EDGE)
        for r in range(ROWS):
            x[HALO + r, to, :] = spread_columns(rim[int(first)], which, r, first)
        for side, pole in ((0, 0), (1, LAT - 1)):

            @pl.when(lat != pole)
            def _():
                for m in range(HALO):
                    x[side * (HALO + ROWS) + m, to, :] = spread_columns(rim[2 + side], which, m + (0 if first else HALO), first)


def grad_kernel(f_own, f_part, p_own, p_part, u_own, u_part, band, g_ref, own_ref, x, rim, basis, ud, g, sems):
    core = my_core()

    def inputs(act):
        fill(act, x, rim, sems, 0, (f_own, f_part), (p_own, p_part), (p_own, p_part), False)
        for core_is, (u0, u1) in enumerate(((u_own, u_part), (u_part, u_own))):
            cols = slice(core_is * HALF, (core_is + 1) * HALF)

            @pl.when(core == core_is)
            def _():
                act(pltpu.make_async_copy(u0.at[:, :, cols], ud.at[0:ROWS], sems.at[FILL_SEMS + 1]))
                act(pltpu.make_async_copy(u1.at[:, :, cols], ud.at[ROWS : 2 * ROWS], sems.at[FILL_SEMS + 2]))

    inputs(start_copy)
    x[EXT : EXT + 1, :, :] = jnp.zeros((1, WIDE, CHANNELS), BF)
    inputs(wait_copy)
    fill_rim(x, rim, 0, 0, EDGE + CHIP)
    for i in range(ROWS):
        for w in range(2):
            cells = x[i : i + TAPS + 1, w * COLS : w * COLS + WIN].reshape(BAND, CHANNELS)
            rows = jnp.dot(band[i], cells, preferred_element_type=F32).astype(BF)
            for k in range(NBASIS):
                basis[k, w * CELLS + i * COLS : w * CELLS + (i + 1) * COLS, :] = rows[k * COLS : (k + 1) * COLS]
    at = pl.multiple_of(core * CELLS, CELLS)
    own_copy = pltpu.make_async_copy(basis.at[:, pl.ds(at, CELLS)], own_ref, sems.at[FILL_SEMS])
    own_copy.start()
    up = ud[...].reshape(2 * CELLS, HALF).T
    outs = []
    for k in range(NBASIS):
        to = slice(k * CHANNELS, (k + 1) * CHANNELS)
        g[to, :] = jnp.dot(up, basis[k], preferred_element_type=F32).astype(BF).T
        outs.append(pltpu.make_async_copy(g.at[to], g_ref.at[to], sems.at[k]))
        outs[-1].start()
    own_copy.wait()
    each(outs, wait_copy)


def tie_kernel(partial, after, out):
    del partial, after, out


def local_kernel(own_ref, w_ref, vec_ref, u_own, u_part, p_own, p_part, a_own, a_part, conv_ref, state_ref, x, rim, bg, acc, sems):
    def inputs(act):
        fill(act, x, rim, sems, 1, (u_own, u_part), (p_own, p_part), (a_own, a_part), True)

    inputs(start_copy)
    total = jnp.zeros((CELLS, CHANNELS), F32)
    for k in range(NBASIS):
        total = total + jnp.dot(own_ref[k], w_ref[k * CHANNELS : (k + 1) * CHANNELS, :], preferred_element_type=F32)
    conv_ref[...] = total.astype(BF).reshape(ROWS, COLS, CHANNELS)
    inputs(wait_copy)

    @pl.when(my_core() == 0)
    def _():
        fill_rim(x, rim, 1, 0, None)

    @pl.when(my_core() == 1)
    def _():
        fill_rim(x, rim, 1, None, WIN - EDGE)

    for k in range(NBASIS):
        wk = w_ref[k * CHANNELS : (k + 1) * CHANNELS, :]
        for part in range(3):
            cells = x[part * 4 : (part + 1) * 4].reshape(4 * WIN, CHANNELS)
            got = lax.dot_general(cells, wk, (((1,), (1,)), ((), ())), preferred_element_type=F32)
            bg[part * 4 : (part + 1) * 4, k * WIN : (k + 1) * WIN, :] = got.astype(BF).reshape(4, WIN, CHANNELS)
    acc[...] = jnp.zeros((ROWS, COLS, CHANNELS), F32)
    for e in range(EXT):
        rows = [r for r in range(ROWS) if 0 <= r + TAPS - 1 - e < TAPS]
        blocks = []
        for r in rows:
            a = r + TAPS - 1 - e
            row = jnp.broadcast_to(vec_ref[a, e : e + 1, :], (COLS, SPAN))
            blocks.append(pltpu.roll(row, 0, 1, stride=1, stride_axis=0).astype(BF))
        got = jnp.dot(jnp.concatenate(blocks, 0), bg[e], preferred_element_type=F32)
        for n, r in enumerate(rows):
            acc[r] += got[n * COLS : (n + 1) * COLS]
    state_ref[...] = acc[...].astype(BF)


def total_kernel(pieces, out):
    for t in range(2):
        out[:, t * HALF : (t + 1) * HALF] = jnp.sum(pieces[:, t].astype(F32), 0)


def on_device(features, upstream, weights, filter_basis, lat_width, lat_offset, lon_reach):
    core = my_core()
    info = jnp.concatenate([lat_width, lat_offset, lon_reach])

    f_part = send(features, to_partner)
    u_part = send(upstream, to_partner)
    own_rows = jnp.where(core == 0, features[ROWS - HALO :], features[:HALO])
    rows = pl.pallas_call(
        rows_kernel,
        out_shape=jax.ShapeDtypeStruct((HALO, CHIP, CHANNELS), BF),
        in_specs=[ANY, ANY],
        out_specs=ANY,
        scratch_shapes=[pltpu.SemaphoreType.DMA((2,))],
        compiler_params=params(4),
        cost_estimate=cost(1000, 2_000_000),
        name="rows",
    )(own_rows, f_part)
    af_own = send(rows, along_meridian)
    filt = jnp.transpose(filter_basis, (2, 3, 0, 1)).reshape(PLACES, NLAT)
    bands, vecs = pl.pallas_call(
        bands_kernel,
        out_shape=(
            jax.ShapeDtypeStruct((ROWS, NBASIS * COLS, BAND), BF),
            jax.ShapeDtypeStruct((TAPS, 16, SPAN), F32),
        ),
        in_specs=[SMEM, VMEM],
        out_specs=(VMEM, VMEM),
        compiler_params=params(16),
        cost_estimate=cost(2_000_000_000, 5_000_000),
        name="bands",
    )(info, filt)

    edges, corners = pl.pallas_call(
        edges_kernel,
        out_shape=(
            jax.ShapeDtypeStruct((PACKED, CHANNELS), BF),
            jax.ShapeDtypeStruct((PACKED, CHANNELS), BF),
        ),
        in_specs=[ANY] * 5,
        out_specs=(VMEM, VMEM),
        scratch_shapes=[
            pltpu.VMEM((2, ROWS, EDGE, CHANNELS), BF),
            pltpu.VMEM((2, 2, HALO, EDGE, CHANNELS), BF),
            pltpu.SemaphoreType.DMA((6,)),
        ],
        compiler_params=params(4),
        cost_estimate=cost(1000, 1_000_000),
        name="edges",
    )(features, f_part, upstream, u_part, vecs)
    e_own = send(edges, to_chip)
    c_own = send(corners, across)
    passed, u_rows = pl.pallas_call(
        relay_kernel,
        out_shape=(
            jax.ShapeDtypeStruct((HALO + 1, CHIP, CHANNELS), BF),
            jax.ShapeDtypeStruct((HALO, CHIP, CHANNELS), BF),
        ),
        in_specs=[ANY] * 5,
        out_specs=(ANY, ANY),
        scratch_shapes=[pltpu.SemaphoreType.DMA((5,))],
        compiler_params=params(4),
        cost_estimate=cost(1000, 4_000_000),
        name="relay",
    )(af_own, e_own, c_own, upstream, u_part)
    p_part = send(passed, to_partner)
    au_own = send(u_rows, along_meridian)
    au_part = send(au_own, to_partner)

    partial, basis_own = pl.pallas_call(
        grad_kernel,
        out_shape=(
            pltpu.HBM((NBASIS * CHANNELS, HALF), BF),
            pltpu.HBM((NBASIS, CELLS, CHANNELS), BF),
        ),
        in_specs=[ANY] * 6 + [VMEM],
        out_specs=(HBM, HBM),
        scratch_shapes=[
            pltpu.VMEM((EXT + 1, WIDE, CHANNELS), BF),
            pltpu.VMEM((4, 2 * EDGE, CHANNELS), BF),
            pltpu.VMEM((NBASIS, 2 * CELLS, CHANNELS), BF),
            pltpu.VMEM((2 * ROWS, COLS, HALF), BF),
            pltpu.VMEM((NBASIS * CHANNELS, HALF), BF),
            pltpu.SemaphoreType.DMA((FILL_SEMS + 3,)),
        ],
        compiler_params=params(20),
        cost_estimate=cost(8_000_000_000, 12_000_000),
        name="grad",
    )(in_hbm(features), in_hbm(f_part), passed, p_part, in_hbm(upstream), in_hbm(u_part), bands)

    partial = pl.pallas_call(
        tie_kernel,
        out_shape=pltpu.HBM(partial.shape, BF),
        in_specs=[HBM, HBM],
        out_specs=HBM,
        input_output_aliases={0: 0},
        compiler_params=params(1),
        name="tie",
    )(partial, au_own)
    pieces = lax.all_to_all(partial.reshape(LAT * LON, OWNED, HALF), BOTH, 0, 0, tiled=True)

    convolved, state_grad = pl.pallas_call(
        local_kernel,
        out_shape=(
            jax.ShapeDtypeStruct((ROWS, COLS, CHANNELS), BF),
            jax.ShapeDtypeStruct((ROWS, COLS, CHANNELS), BF),
        ),
        in_specs=[VMEM] * 3 + [ANY] * 6,
        out_specs=(VMEM, VMEM),
        scratch_shapes=[
            pltpu.VMEM((EXT, WIN, CHANNELS), BF),
            pltpu.VMEM((4, 2 * EDGE, CHANNELS), BF),
            pltpu.VMEM((EXT, SPAN, CHANNELS), BF),
            pltpu.VMEM((ROWS, COLS, CHANNELS), F32),
            pltpu.SemaphoreType.DMA((FILL_SEMS,)),
        ],
        compiler_params=params(28),
        cost_estimate=cost(10_000_000_000, 12_000_000),
        name="local",
    )(basis_own, weights, vecs, upstream, u_part, passed, p_part, au_own, au_part)

    weight_grad = pl.pallas_call(
        total_kernel,
        out_shape=jax.ShapeDtypeStruct((OWNED, CHANNELS), F32),
        in_specs=[VMEM],
        out_specs=VMEM,
        compiler_params=params(16),
        name="total",
    )(pltpu.with_memory_space_constraint(pieces.reshape(LAT * LON // 2, 2, OWNED, HALF), pltpu.VMEM))
    return convolved, state_grad, weight_grad


def solution(mesh):
    return jax.shard_map(
        on_device,
        mesh=mesh,
        in_specs=(P("lat", "lon", None), P("lat", "lon", None), P(), P(), P(), P(), P()),
        out_specs=(P("lat", "lon", None), P("lat", "lon", None), P(("lat", "lon"), None)),
        check_vma=False,
    )
```

```python
import jax
import jax.numpy as jnp
from jax import lax
from jax.experimental import pallas as pl
from jax.experimental.pallas import tpu as pltpu
from jax.sharding import PartitionSpec as P

CHANNELS = 768
NBASIS = 4
HALO = 3
TAPS = 7
LAT = 32
LON = 4
NLAT = 192
ROWS = 6
COLS = 64
EDGE = 16
WIN = COLS + 2 * EDGE
CHIP = 2 * COLS
WIDE = CHIP + 2 * EDGE
EXT = ROWS + 2 * HALO
HALF = CHANNELS // 2
CELLS = ROWS * COLS
BAND = (TAPS + 1) * WIN
SPAN = NBASIS * WIN
OUTER = ROWS * EDGE + HALO * WIN
TALL = ROWS * NBASIS * COLS
PLACES = TAPS * TAPS * NBASIS
OWNED = NBASIS * CHANNELS // (LAT * LON)
BF = jnp.bfloat16
F32 = jnp.float32
BOTH = ("lat", "lon")
DEVICES = [(lat, lon) for lat in range(LAT) for lon in range(LON)]

VMEM = pl.BlockSpec(memory_space=pltpu.VMEM)
SMEM = pl.BlockSpec(memory_space=pltpu.SMEM)
ANY = pl.BlockSpec(memory_space=pl.ANY)
HBM = pl.BlockSpec(memory_space=pltpu.HBM)
MIB = 1024 * 1024


def params(mib):
    return pltpu.CompilerParams(vmem_limit_bytes=mib * MIB)


def in_hbm(block):
    return pltpu.with_memory_space_constraint(block, pltpu.HBM)


def cost(flops, size):
    return pl.CostEstimate(flops=flops, bytes_accessed=size, transcendentals=0)


def send(block, move):
    pairs = []
    for lat, lon in DEVICES:
        to = move(lat, lon)
        if to is not None:
            pairs.append((lat * LON + lon, to[0] * LON + to[1]))
    return lax.ppermute(block, BOTH, pairs)


def to_partner(lat, lon):
    return lat, lon ^ 1


def to_chip(lat, lon):
    return lat, lon ^ 2


def along_meridian(lat, lon):
    if lon % 2 == 0:
        return (lat + 1, lon) if lat + 1 < LAT else (lat, lon ^ 3)
    return (lat - 1, lon) if lat > 0 else (lat, lon ^ 3)


def across(lat, lon):
    to_lat = lat + 1 if lon % 2 == 0 else lat - 1
    return (to_lat, lon ^ 2) if 0 <= to_lat < LAT else None


def split(values, size):
    high = jnp.floor((values.astype(F32) + 0.5) * (1.0 / size)).astype(jnp.int32)
    return high, values - high * size


def bands_kernel(info, filt, inner_ref, outer_ref, vec_ref):
    lat = my_lat()
    lane = lax.broadcasted_iota(jnp.int32, (1, 128), 1)
    row_of = lat * ROWS + lane - HALO
    row_of = jnp.where(row_of < 0, -1 - row_of, row_of)
    row_of = jnp.where(row_of >= NLAT, 2 * NLAT - 1 - row_of, row_of)
    pick = lax.broadcasted_iota(jnp.int32, (NLAT, 128), 0) == row_of
    rows = jnp.dot(filt[...], pick.astype(F32).astype(BF), preferred_element_type=F32)
    low = jnp.zeros((1, 128), jnp.int32)
    high = jnp.zeros((1, 128), jnp.int32)
    far = jnp.zeros((1, 128), jnp.int32)
    for e in range(EXT):
        row = lat * ROWS + e - HALO
        row = jnp.where(row < 0, -1 - row, row)
        row = jnp.where(row >= NLAT, 2 * NLAT - 1 - row, row)
        width, offset, reach = info[row], info[NLAT + row], info[2 * NLAT + row]
        low = jnp.where(lane == e, offset, low)
        high = jnp.where(lane == e, offset + width, high)
        far = jnp.where(lane == e, reach, far)
    a, rest = split(lax.broadcasted_iota(jnp.int32, (PLACES, 128), 0), TAPS * NBASIS)
    b, _ = split(rest, NBASIS)
    keep = (a >= low) & (a < high) & (jnp.abs(b - HALO) <= far)
    rows = jnp.where(keep, rows, 0.0).astype(BF)
    over = (((0,), (0,)), ((), ()))
    a, b = split(lax.broadcasted_iota(jnp.int32, (1, BAND), 1), WIN)
    b = b - (EDGE - HALO)
    band_at = jnp.where((a < TAPS) & (b >= 0) & (b < TAPS), (a * TAPS + b) * NBASIS, -PLACES)
    place = lax.broadcasted_iota(jnp.int32, (PLACES, BAND), 0)
    edge_a, edge_q = split(lax.broadcasted_iota(jnp.int32, (1, 128), 1), EDGE)
    edge_place = lax.broadcasted_iota(jnp.int32, (PLACES, 128), 0)
    edge_at = []
    for w in range(2):
        b = edge_q - (EDGE - HALO) if w == 0 else edge_q + HALO + 1
        ok = (edge_a < TAPS) & (b >= 0) & (b < TAPS)
        edge_at.append(jnp.where(ok, (edge_a * TAPS + b) * NBASIS, -PLACES))
    j = lax.broadcasted_iota(jnp.int32, (COLS, 128), 0)
    _, q = split(lax.broadcasted_iota(jnp.int32, (COLS, 128), 1), EDGE)
    inside = (q >= EDGE - HALO + j, q <= j - (COLS - HALO))
    in_edge = lax.broadcasted_iota(jnp.int32, (COLS, 128), 1) < ROWS * EDGE

    def turned(vec, i, keep, shift, width):
        row = jnp.where(keep, vec[HALO + i : HALO + i + 1, :], 0.0)
        return pltpu.roll(jnp.broadcast_to(row, (COLS, width)), shift % width, 1, stride=1, stride_axis=0)

    for k in range(NBASIS):
        put = (place == band_at + k).astype(F32).astype(BF)
        vec = lax.dot_general(rows, put, over, preferred_element_type=F32)
        edge_vec = []
        for w in range(2):
            put = (edge_place == edge_at[w] + k).astype(F32).astype(BF)
            edge_vec.append(lax.dot_general(rows, put, over, preferred_element_type=F32))
        for i in range(ROWS):
            to = slice((i * NBASIS + k) * COLS, (i * NBASIS + k + 1) * COLS)
            keep = (a >= HALO - i) & (a < HALO + ROWS - i)
            inner_ref[to, :] = turned(vec, i, keep, (i - HALO) * WIN, BAND).astype(BF)
            keep = (a < HALO - i) if i < HALO else (a >= HALO + ROWS - i)
            rim = turned(vec, i, keep, (1 + i if i < HALO else i - TAPS - 1) * WIN, BAND)
            keep = (edge_a >= HALO - i) & (edge_a < HALO + ROWS - i)
            for w in range(2):
                edge = turned(edge_vec[w], i, keep, (i - HALO) * EDGE - w * (COLS - 1), 128)
                edge = jnp.where(inside[w], edge, 0.0)
                outer_ref[w, to, 0:128] = jnp.where(in_edge, edge, rim[:, 0:128]).astype(BF)
                outer_ref[w, to, 128:OUTER] = rim[:, 128:OUTER].astype(BF)
    k, b = split(lax.broadcasted_iota(jnp.int32, (1, SPAN), 1), WIN)
    b = EDGE + HALO - b
    spread_at = jnp.where((b >= 0) & (b < TAPS), b * NBASIS + k, -PLACES)
    place = lax.broadcasted_iota(jnp.int32, (PLACES, SPAN), 0)
    vecs = []
    for a in range(TAPS):
        put = (place == spread_at + a * TAPS * NBASIS).astype(F32).astype(BF)
        vecs.append(lax.dot_general(rows, put, over, preferred_element_type=F32)[:16])
    e = lax.broadcasted_iota(jnp.int32, (16, SPAN), 0)
    beyond = ((lat == 0) & (e < HALO)) | ((lat == LAT - 1) & (e >= HALO + ROWS))
    for a in range(TAPS):
        vec_ref[a] = jnp.where(beyond, vecs[TAPS - 1 - a], vecs[a])


def each(todo, act):
    for c in todo:
        act(c)


def start_copy(c):
    c.start()


def wait_copy(c):
    c.wait()


def my_core():
    return lax.rem(lax.axis_index("lon"), 2)


def my_lat():
    return lax.axis_index("lat")


def run(todo):
    each(todo, start_copy)
    each(todo, wait_copy)


def row_copies(sources, out, sems, turn):
    todo = []
    for n, (ref, row, columns) in enumerate(sources):
        if turn:
            for m in range(HALO):
                todo.append(pltpu.make_async_copy(ref.at[row + HALO - 1 - m], out.at[m, columns], sems.at[HALO * n + m]))
        else:
            todo.append(pltpu.make_async_copy(ref.at[row : row + HALO], out.at[:, columns], sems.at[HALO * n]))
    return todo


def chip_rows(own, own_row, part, out, sems, act):
    low, high = slice(0, COLS), slice(COLS, CHIP)
    for core_is, row, pole in ((0, ROWS - HALO, LAT - 1), (1, 0, 0)):
        mine, other = (low, high) if core_is == 0 else (high, low)
        sources = ((own, row if own_row is None else own_row, mine), (part, row, other))
        for turn in (False, True):

            @pl.when((my_core() == core_is) & ((my_lat() == pole) == turn))
            def _():
                each(row_copies(sources, out, sems, turn), act)


def rows_kernel(own, part, out, sems):
    chip_rows(own, 0, part, out, sems, start_copy)
    chip_rows(own, 0, part, out, sems, wait_copy)


def relay_kernel(a_own, e_own, c_own, u_rows, out, u_out, sems):
    del u_rows, u_out
    run(
        [
            pltpu.make_async_copy(a_own, out.at[0:HALO], sems.at[0]),
            pltpu.make_async_copy(e_own, out.at[HALO, 0:PACKED], sems.at[1]),
            pltpu.make_async_copy(c_own, out.at[HALO, COLS : COLS + PACKED], sems.at[2]),
        ]
    )


PACKED = 3 * EDGE


def gather_columns(rows, firsts):
    slot = lax.broadcasted_iota(jnp.int32, (EDGE, CHANNELS), 0)
    out = jnp.zeros((EDGE, CHANNELS), F32)
    for m, (row, first) in enumerate(zip(rows, firsts)):
        shift = (4 * m - (0 if first else EDGE - HALO)) % EDGE
        moved = pltpu.roll(row.astype(F32), shift, 0)
        out = jnp.where((slot >= 4 * m) & (slot < 4 * m + HALO), moved, out)
    return out.astype(BF)


def pack_columns(out, rows, firsts):
    for g in range(3):
        four = slice(4 * g, 4 * g + 4)
        out[g * EDGE : (g + 1) * EDGE] = gather_columns(rows[four], firsts[four])


def spread_columns(rim, which, row, first):
    at = 2 * HALO * which + row
    block, m = at // 4 - which, at % 4
    slot = lax.broadcasted_iota(jnp.int32, (EDGE, CHANNELS), 0)
    shift = ((0 if first else EDGE - HALO) - 4 * m) % EDGE
    moved = pltpu.roll(rim[block * EDGE : (block + 1) * EDGE].astype(F32), shift, 0)
    keep = slot < HALO if first else slot >= EDGE - HALO
    return jnp.where(keep, moved, 0.0).astype(BF)


def edges_kernel(f_own, f_part, u_own, u_part, edge, corner, outer, sides, sems):
    first, last = slice(0, EDGE), slice(COLS - EDGE, COLS)

    def copies(columns, row, halves):
        todo = []
        for n, (own, half0, half1) in enumerate(halves):
            at = pl.ds(row, HALO)
            todo.append(pltpu.make_async_copy(own.at[:, columns], outer.at[n], sems.at[3 * n]))
            todo.append(pltpu.make_async_copy(half0.at[at, first], sides.at[n, 0], sems.at[3 * n + 1]))
            todo.append(pltpu.make_async_copy(half1.at[at, last], sides.at[n, 1], sems.at[3 * n + 2]))
        return todo

    @pl.when(my_core() == 0)
    def _():
        run(copies(first, ROWS - HALO, ((f_own, f_own, f_part), (u_own, u_own, u_part))))
        pack_columns(edge, [outer[n, r] for n in range(2) for r in range(ROWS)], [True] * (2 * ROWS))

    @pl.when(my_core() == 1)
    def _():
        run(copies(last, 0, ((f_own, f_part, f_own), (u_own, u_part, u_own))))
        pack_columns(edge, [outer[n, r] for n in range(2) for r in range(ROWS)], [False] * (2 * ROWS))

    places = [(n, side, m) for n in range(2) for side in range(2) for m in range(HALO)]
    pack_columns(corner, [sides[at] for at in places], [side == 0 for _, side, _ in places])


def fill_copies(x, rim, sems, which, lat_is, half0, half1, passed0, passed1, rows0, rows1, start, stop):
    todo = []

    def put(ref, columns, at, rows, n):
        low, high = max(at, start), min(at + columns.stop - columns.start, stop)
        if low < high:
            src = ref.at[:, columns.start + low - at : columns.start + high - at]
            todo.append(pltpu.make_async_copy(src, x.at[rows, low - start : high - start], sems.at[n]))

    def put_row(ref, row, columns, at, to, n):
        low, high = max(at, start), min(at + columns.stop - columns.start, stop)
        if low < high:
            src = ref.at[row, columns.start + low - at : columns.start + high - at]
            todo.append(pltpu.make_async_copy(src, x.at[to, low - start : high - start], sems.at[n]))

    whole, first, last = slice(0, COLS), slice(0, EDGE), slice(COLS - EDGE, COLS)
    left, right = 0, EDGE + CHIP
    mid = slice(HALO, HALO + ROWS)
    for n, (ref, at) in enumerate(((passed1, 0), (passed0, 0), (passed0, COLS), (passed1, COLS))):
        at += EDGE * which
        todo.append(pltpu.make_async_copy(ref.at[HALO, at : at + 2 * EDGE], rim.at[n], sems.at[n]))
    put(half0, whole, EDGE, mid, 4)
    put(half1, whole, EDGE + COLS, mid, 5)
    n = 6
    for side, rows in enumerate((rows0, rows1)):
        to = side * (HALO + ROWS)
        if lat_is == side:
            for m in range(HALO):
                own = HALO - 1 - m + side * (ROWS - HALO)
                put_row(half1, own, last, left, to + m, n + 2 * m + 1)
                put_row(half0, own, first, right, to + m, n + 2 * m + 2)
        put(rows.at[0:HALO], slice(0, CHIP), EDGE, slice(to, to + HALO), n)
        n += 7
    return todo


FILL_SEMS = 20


def fill(act, x, rim, sems, which, half, passed, rows):
    core, lat = my_core(), my_lat()
    for core_is in range(2):
        refs = [pair[core_is ^ c] for pair in (half, passed, rows) for c in range(2)]
        start, stop = core_is * COLS, core_is * COLS + WIN
        for lat_is, here in ((0, lat == 0), (1, lat == LAT - 1), (None, (lat > 0) & (lat < LAT - 1))):

            @pl.when((core == core_is) & here)
            def _():
                each(fill_copies(x, rim, sems, which, lat_is, *refs, start, stop), act)


def fill_rim(x, rim, which, left, right):
    lat = my_lat()
    for at, first in ((left, False), (right, True)):
        if at is None:
            continue
        to = slice(at, at + EDGE)
        for r in range(ROWS):
            x[HALO + r, to, :] = spread_columns(rim[int(first)], which, r, first)
        for side, pole in ((0, 0), (1, LAT - 1)):

            @pl.when(lat != pole)
            def _():
                for m in range(HALO):
                    x[side * (HALO + ROWS) + m, to, :] = spread_columns(rim[2 + side], which, m + (0 if first else HALO), first)


def inner_kernel(f_own, f_part, u_own, u_part, band, acc, up_ref, pole_ref, u_rows, x, ud, sems, row_sems):
    core = my_core()
    chip_rows(u_own, None, u_part, u_rows, row_sems, start_copy)

    def inputs(act):
        for core_is, (f0, f1, u0, u1) in enumerate(((f_own, f_part, u_own, u_part), (f_part, f_own, u_part, u_own))):
            cols = slice(core_is * HALF, (core_is + 1) * HALF)

            @pl.when(core == core_is)
            def _():
                act(pltpu.make_async_copy(f0, x.at[0:ROWS, EDGE : EDGE + COLS], sems.at[0]))
                act(pltpu.make_async_copy(f1, x.at[0:ROWS, EDGE + COLS : EDGE + CHIP], sems.at[1]))
                act(pltpu.make_async_copy(u0.at[:, :, cols], ud.at[0:ROWS], sems.at[2]))
                act(pltpu.make_async_copy(u1.at[:, :, cols], ud.at[ROWS : 2 * ROWS], sems.at[3]))

    inputs(start_copy)
    x[0:ROWS, 0:EDGE, :] = jnp.zeros((ROWS, EDGE, CHANNELS), BF)
    x[0:ROWS, EDGE + CHIP :, :] = jnp.zeros((ROWS, EDGE, CHANNELS), BF)
    x[ROWS:, :, :] = jnp.zeros((2, WIDE, CHANNELS), BF)
    inputs(wait_copy)
    shift = jnp.where(my_lat() == LAT - 1, ROWS - HALO, 0)
    for m in range(HALO):
        row = HALO - 1 - m + shift
        pole_ref[0, m] = x[row, CHIP : CHIP + EDGE, :]
        pole_ref[1, m] = x[row, EDGE : 2 * EDGE, :]
    for w in range(2):
        cells = x[:, w * COLS : w * COLS + WIN].reshape(BAND, CHANNELS)
        for part in range(3):
            to = slice(part * (TALL // 3), (part + 1) * (TALL // 3))
            acc[w, to] = jnp.dot(band[to], cells, preferred_element_type=F32)
    up_ref[...] = ud[...].reshape(2 * CELLS, HALF).T
    chip_rows(u_own, None, u_part, u_rows, row_sems, wait_copy)


def outer_copies(x, rim, sems, passed0, passed1):
    todo = []
    for n, (ref, at) in enumerate(((passed1, 0), (passed0, 0), (passed0, COLS), (passed1, COLS))):
        todo.append(pltpu.make_async_copy(ref.at[HALO, at : at + 2 * EDGE], rim.at[n], sems.at[n]))
    low, high = slice(0, WIN - EDGE), slice(CHIP - WIN + EDGE, CHIP)
    for side, rows in enumerate((passed0, passed1)):
        n = 4 + 2 * side
        todo.append(pltpu.make_async_copy(rows.at[0:HALO, low], x.at[side, 0, 1 : 1 + HALO, EDGE:WIN], sems.at[n]))
        todo.append(pltpu.make_async_copy(rows.at[0:HALO, high], x.at[side, 1, 1 : 1 + HALO, 0 : WIN - EDGE], sems.at[n + 1]))
    return todo


OUTER_SEMS = 8


def grad_kernel(p_own, p_part, pole_ref, acc, band, up, g_ref, own_ref, x, rim, basis, g, sems):
    core, lat = my_core(), my_lat()

    def inputs(act):
        for core_is, refs in enumerate(((p_own, p_part), (p_part, p_own))):

            @pl.when(core == core_is)
            def _():
                each(outer_copies(x, rim, sems, *refs), act)

    inputs(start_copy)
    inputs(wait_copy)
    for w, first in ((0, False), (1, True)):
        for r in range(ROWS):
            columns = spread_columns(rim[w], 0, r, first)
            for side in range(2):
                x[side, w, 0, r * EDGE : (r + 1) * EDGE, :] = columns
        at = w * (WIN - EDGE)
        for side, pole in ((0, 0), (1, LAT - 1)):

            @pl.when(lat != pole)
            def _():
                for m in range(HALO):
                    x[side, w, 1 + m, at : at + EDGE, :] = spread_columns(rim[2 + side], 0, m + (0 if first else HALO), first)

            @pl.when(lat == pole)
            def _():
                for m in range(HALO):
                    x[side, w, 1 + m, at : at + EDGE, :] = pole_ref[w, m]

    for side in range(2):
        to = slice(side * (TALL // 2), (side + 1) * (TALL // 2))
        for w in range(2):
            cells = x[side, w].reshape(OUTER, CHANNELS)
            rows = (acc[w, to] + jnp.dot(band[w, to], cells, preferred_element_type=F32)).astype(BF)
            for m in range(HALO):
                at = w * CELLS + (side * HALO + m) * COLS
                for k in range(NBASIS):
                    n = (m * NBASIS + k) * COLS
                    basis[k, at : at + COLS, :] = rows[n : n + COLS]
    at = pl.multiple_of(core * CELLS, CELLS)
    own_copy = pltpu.make_async_copy(basis.at[:, pl.ds(at, CELLS)], own_ref, sems.at[4])
    own_copy.start()
    outs = []
    for k in range(NBASIS):
        to = slice(k * CHANNELS, (k + 1) * CHANNELS)
        g[to, :] = jnp.dot(up[...], basis[k], preferred_element_type=F32).astype(BF).T
        outs.append(pltpu.make_async_copy(g.at[to], g_ref.at[to], sems.at[k]))
        outs[-1].start()
    own_copy.wait()
    each(outs, wait_copy)


def tie_kernel(rows, after, out):
    del rows, after, out


def conv_kernel(own_ref, w_ref, conv_ref):
    total = jnp.zeros((CELLS, CHANNELS), F32)
    for k in range(NBASIS):
        total = total + jnp.dot(own_ref[k], w_ref[k * CHANNELS : (k + 1) * CHANNELS, :], preferred_element_type=F32)
    conv_ref[...] = total.astype(BF).reshape(ROWS, COLS, CHANNELS)


def state_kernel(w_ref, vec_ref, u_own, u_part, p_own, p_part, a_own, a_part, state_ref, x, rim, bg, acc, sems):
    def inputs(act):
        fill(act, x, rim, sems, 1, (u_own, u_part), (p_own, p_part), (a_own, a_part))

    inputs(start_copy)
    inputs(wait_copy)

    @pl.when(my_core() == 0)
    def _():
        fill_rim(x, rim, 1, 0, None)

    @pl.when(my_core() == 1)
    def _():
        fill_rim(x, rim, 1, None, WIN - EDGE)

    for k in range(NBASIS):
        wk = w_ref[k * CHANNELS : (k + 1) * CHANNELS, :]
        for part in range(3):
            cells = x[part * 4 : (part + 1) * 4].reshape(4 * WIN, CHANNELS)
            got = lax.dot_general(cells, wk, (((1,), (1,)), ((), ())), preferred_element_type=F32)
            bg[part * 4 : (part + 1) * 4, k * WIN : (k + 1) * WIN, :] = got.astype(BF).reshape(4, WIN, CHANNELS)
    acc[...] = jnp.zeros((ROWS, COLS, CHANNELS), F32)
    for e in range(EXT):
        rows = [r for r in range(ROWS) if 0 <= r + TAPS - 1 - e < TAPS]
        blocks = []
        for r in rows:
            a = r + TAPS - 1 - e
            row = jnp.broadcast_to(vec_ref[a, e : e + 1, :], (COLS, SPAN))
            blocks.append(pltpu.roll(row, 0, 1, stride=1, stride_axis=0).astype(BF))
        got = jnp.dot(jnp.concatenate(blocks, 0), bg[e], preferred_element_type=F32)
        for n, r in enumerate(rows):
            acc[r] += got[n * COLS : (n + 1) * COLS]
    state_ref[...] = acc[...].astype(BF)


def total_kernel(pieces, out):
    for t in range(2):
        out[:, t * HALF : (t + 1) * HALF] = jnp.sum(pieces[:, t].astype(F32), 0)


def on_device(features, upstream, weights, filter_basis, lat_width, lat_offset, lon_reach):
    core = my_core()
    info = jnp.concatenate([lat_width, lat_offset, lon_reach])

    f_part = send(features, to_partner)
    u_part = send(upstream, to_partner)
    own_rows = jnp.where(core == 0, features[ROWS - HALO :], features[:HALO])
    rows = pl.pallas_call(
        rows_kernel,
        out_shape=jax.ShapeDtypeStruct((HALO, CHIP, CHANNELS), BF),
        in_specs=[ANY, ANY],
        out_specs=ANY,
        scratch_shapes=[pltpu.SemaphoreType.DMA((2 * HALO,))],
        compiler_params=params(4),
        cost_estimate=cost(1000, 2_000_000),
        name="rows",
    )(own_rows, f_part)
    af_own = send(rows, along_meridian)
    filt = jnp.transpose(filter_basis, (2, 3, 0, 1)).reshape(PLACES, NLAT)
    inner_band, outer_band, vecs = pl.pallas_call(
        bands_kernel,
        out_shape=(
            jax.ShapeDtypeStruct((TALL, BAND), BF),
            jax.ShapeDtypeStruct((2, TALL, OUTER), BF),
            jax.ShapeDtypeStruct((TAPS, 16, SPAN), F32),
        ),
        in_specs=[SMEM, VMEM],
        out_specs=(VMEM, VMEM, VMEM),
        compiler_params=params(16),
        cost_estimate=cost(2_000_000_000, 5_000_000),
        name="bands",
    )(info, filt)

    edges, corners = pl.pallas_call(
        edges_kernel,
        out_shape=(
            jax.ShapeDtypeStruct((PACKED, CHANNELS), BF),
            jax.ShapeDtypeStruct((PACKED, CHANNELS), BF),
        ),
        in_specs=[ANY] * 4,
        out_specs=(VMEM, VMEM),
        scratch_shapes=[
            pltpu.VMEM((2, ROWS, EDGE, CHANNELS), BF),
            pltpu.VMEM((2, 2, HALO, EDGE, CHANNELS), BF),
            pltpu.SemaphoreType.DMA((6,)),
        ],
        compiler_params=params(4),
        cost_estimate=cost(1000, 1_000_000),
        name="edges",
    )(features, f_part, upstream, u_part)
    e_own = send(edges, to_chip)
    c_own = send(corners, across)
    acc, up, pole, u_rows = pl.pallas_call(
        inner_kernel,
        out_shape=(
            jax.ShapeDtypeStruct((2, TALL, CHANNELS), F32),
            jax.ShapeDtypeStruct((HALF, 2 * CELLS), BF),
            jax.ShapeDtypeStruct((2, HALO, EDGE, CHANNELS), BF),
            jax.ShapeDtypeStruct((HALO, CHIP, CHANNELS), BF),
        ),
        in_specs=[ANY] * 4 + [VMEM],
        out_specs=(VMEM, VMEM, VMEM, ANY),
        scratch_shapes=[
            pltpu.VMEM((ROWS + 2, WIDE, CHANNELS), BF),
            pltpu.VMEM((2 * ROWS, COLS, HALF), BF),
            pltpu.SemaphoreType.DMA((4,)),
            pltpu.SemaphoreType.DMA((2 * HALO,)),
        ],
        compiler_params=params(28),
        cost_estimate=cost(4_000_000_000, 16_000_000),
        name="inner",
    )(features, f_part, upstream, u_part, inner_band)
    passed, u_rows = pl.pallas_call(
        relay_kernel,
        out_shape=(
            jax.ShapeDtypeStruct((HALO + 1, CHIP, CHANNELS), BF),
            jax.ShapeDtypeStruct((HALO, CHIP, CHANNELS), BF),
        ),
        in_specs=[ANY] * 4,
        out_specs=(ANY, ANY),
        input_output_aliases={3: 1},
        scratch_shapes=[pltpu.SemaphoreType.DMA((3,))],
        compiler_params=params(4),
        cost_estimate=cost(1000, 4_000_000),
        name="relay",
    )(af_own, e_own, c_own, u_rows)
    p_part = send(passed, to_partner)
    au_own = send(u_rows, along_meridian)
    partial, basis_own = pl.pallas_call(
        grad_kernel,
        out_shape=(
            pltpu.HBM((NBASIS * CHANNELS, HALF), BF),
            pltpu.HBM((NBASIS, CELLS, CHANNELS), BF),
        ),
        in_specs=[ANY] * 2 + [VMEM] * 4,
        out_specs=(HBM, HBM),
        scratch_shapes=[
            pltpu.VMEM((2, 2, 1 + HALO, WIN, CHANNELS), BF),
            pltpu.VMEM((4, 2 * EDGE, CHANNELS), BF),
            pltpu.VMEM((NBASIS, 2 * CELLS, CHANNELS), BF),
            pltpu.VMEM((NBASIS * CHANNELS, HALF), BF),
            pltpu.SemaphoreType.DMA((OUTER_SEMS,)),
        ],
        compiler_params=params(30),
        cost_estimate=cost(6_000_000_000, 12_000_000),
        name="grad",
    )(passed, p_part, pole, acc, outer_band, up)

    pieces = lax.all_to_all(partial.reshape(LAT * LON, OWNED, HALF), BOTH, 0, 0, tiled=True)

    convolved = pl.pallas_call(
        conv_kernel,
        out_shape=jax.ShapeDtypeStruct((ROWS, COLS, CHANNELS), BF),
        in_specs=[VMEM] * 2,
        out_specs=VMEM,
        compiler_params=params(20),
        cost_estimate=cost(80_000_000_000, 8_000_000),
        name="conv",
    )(basis_own, weights)
    au_own = pl.pallas_call(
        tie_kernel,
        out_shape=jax.ShapeDtypeStruct(au_own.shape, BF),
        in_specs=[ANY, ANY],
        out_specs=ANY,
        input_output_aliases={0: 0},
        compiler_params=params(1),
        name="tie",
    )(au_own, in_hbm(convolved))
    au_part = send(au_own, to_partner)
    state_grad = pl.pallas_call(
        state_kernel,
        out_shape=jax.ShapeDtypeStruct((ROWS, COLS, CHANNELS), BF),
        in_specs=[VMEM] * 2 + [ANY] * 6,
        out_specs=VMEM,
        scratch_shapes=[
            pltpu.VMEM((EXT, WIN, CHANNELS), BF),
            pltpu.VMEM((4, 2 * EDGE, CHANNELS), BF),
            pltpu.VMEM((EXT, SPAN, CHANNELS), BF),
            pltpu.VMEM((ROWS, COLS, CHANNELS), F32),
            pltpu.SemaphoreType.DMA((FILL_SEMS,)),
        ],
        compiler_params=params(28),
        cost_estimate=cost(8_000_000_000, 12_000_000),
        name="state",
    )(weights, vecs, upstream, u_part, passed, p_part, au_own, au_part)

    weight_grad = pl.pallas_call(
        total_kernel,
        out_shape=jax.ShapeDtypeStruct((OWNED, CHANNELS), F32),
        in_specs=[VMEM],
        out_specs=VMEM,
        compiler_params=params(16),
        name="total",
    )(pltpu.with_memory_space_constraint(pieces.reshape(LAT * LON // 2, 2, OWNED, HALF), pltpu.VMEM))
    return convolved, state_grad, weight_grad


def solution(mesh):
    return jax.shard_map(
        on_device,
        mesh=mesh,
        in_specs=(P("lat", "lon", None), P("lat", "lon", None), P(), P(), P(), P(), P()),
        out_specs=(P("lat", "lon", None), P("lat", "lon", None), P(("lat", "lon"), None)),
        check_vma=False,
    )
```

```python
import jax
import jax.numpy as jnp
from jax import lax
from jax.experimental import pallas as pl
from jax.experimental.pallas import tpu as pltpu
from jax.sharding import PartitionSpec as P

CHANNELS = 768
NBASIS = 4
HALO = 3
TAPS = 7
LAT = 32
LON = 4
NLAT = 192
ROWS = 6
COLS = 64
EDGE = 16
WIN = COLS + 2 * EDGE
CHIP = 2 * COLS
WIDE = CHIP + 2 * EDGE
EXT = ROWS + 2 * HALO
HALF = CHANNELS // 2
CELLS = ROWS * COLS
BAND = (TAPS + 1) * WIN
SPAN = NBASIS * WIN
OUTER = (HALO + 1) * WIN
TALL = ROWS * NBASIS * COLS
PLACES = TAPS * TAPS * NBASIS
OWNED = NBASIS * CHANNELS // (LAT * LON)
BF = jnp.bfloat16
F32 = jnp.float32
BOTH = ("lat", "lon")
DEVICES = [(lat, lon) for lat in range(LAT) for lon in range(LON)]

VMEM = pl.BlockSpec(memory_space=pltpu.VMEM)
SMEM = pl.BlockSpec(memory_space=pltpu.SMEM)
ANY = pl.BlockSpec(memory_space=pl.ANY)
HBM = pl.BlockSpec(memory_space=pltpu.HBM)
MIB = 1024 * 1024


def params(mib):
    return pltpu.CompilerParams(vmem_limit_bytes=mib * MIB)


def in_hbm(block):
    return pltpu.with_memory_space_constraint(block, pltpu.HBM)


def cost(flops, size):
    return pl.CostEstimate(flops=flops, bytes_accessed=size, transcendentals=0)


def send(block, move):
    pairs = []
    for lat, lon in DEVICES:
        to = move(lat, lon)
        if to is not None:
            pairs.append((lat * LON + lon, to[0] * LON + to[1]))
    return lax.ppermute(block, BOTH, pairs)


def to_partner(lat, lon):
    return lat, lon ^ 1


def to_chip(lat, lon):
    return lat, lon ^ 2


def along_meridian(lat, lon):
    if lon % 2 == 0:
        return (lat + 1, lon) if lat + 1 < LAT else (lat, lon ^ 3)
    return (lat - 1, lon) if lat > 0 else (lat, lon ^ 3)


def across(lat, lon):
    to_lat = lat + 1 if lon % 2 == 0 else lat - 1
    return (to_lat, lon ^ 2) if 0 <= to_lat < LAT else None


def split(values, size):
    high = jnp.floor((values.astype(F32) + 0.5) * (1.0 / size)).astype(jnp.int32)
    return high, values - high * size


def outer_rows(i):
    return ((0, 384), (96, 256), (192, 128), (64, 128), (64, 256), (0, 384))[i]


def outer_lanes(i):
    first = outer_rows(i)[0]
    if i < HALO:
        return i * WIN - first, HALO * WIN - first
    return WIN - first, WIN - 2 * EDGE - first


def masked_filters(info, filt):
    lat = my_lat()
    lane = lax.broadcasted_iota(jnp.int32, (1, 128), 1)
    row_of = lat * ROWS + lane - HALO
    row_of = jnp.where(row_of < 0, -1 - row_of, row_of)
    row_of = jnp.where(row_of >= NLAT, 2 * NLAT - 1 - row_of, row_of)
    pick = lax.broadcasted_iota(jnp.int32, (NLAT, 128), 0) == row_of
    rows = jnp.dot(filt[...], pick.astype(F32).astype(BF), preferred_element_type=F32)
    low = jnp.zeros((1, 128), jnp.int32)
    high = jnp.zeros((1, 128), jnp.int32)
    far = jnp.zeros((1, 128), jnp.int32)
    for e in range(EXT):
        row = lat * ROWS + e - HALO
        row = jnp.where(row < 0, -1 - row, row)
        row = jnp.where(row >= NLAT, 2 * NLAT - 1 - row, row)
        width, offset, reach = info[row], info[NLAT + row], info[2 * NLAT + row]
        low = jnp.where(lane == e, offset, low)
        high = jnp.where(lane == e, offset + width, high)
        far = jnp.where(lane == e, reach, far)
    a, rest = split(lax.broadcasted_iota(jnp.int32, (PLACES, 128), 0), TAPS * NBASIS)
    b, _ = split(rest, NBASIS)
    keep = (a >= low) & (a < high) & (jnp.abs(b - HALO) <= far)
    return jnp.where(keep, rows, 0.0).astype(BF)


OVER_ROWS = (((0,), (0,)), ((), ()))


def bands_kernel(info, filt, inner_ref, outer_ref):
    rows = masked_filters(info, filt)
    a, b = split(lax.broadcasted_iota(jnp.int32, (1, BAND), 1), WIN)
    b = b - (EDGE - HALO)
    band_at = jnp.where((a < TAPS) & (b >= 0) & (b < TAPS), (a * TAPS + b) * NBASIS, -PLACES)
    place = lax.broadcasted_iota(jnp.int32, (PLACES, BAND), 0)
    edge_a, edge_c = split(lax.broadcasted_iota(jnp.int32, (1, 128), 1), 4)
    edge_place = lax.broadcasted_iota(jnp.int32, (PLACES, 128), 0)
    edge_at = []
    for w in range(2):
        b = edge_c + w * (HALO + 1)
        ok = (edge_a < TAPS) & (edge_c < HALO)
        edge_at.append(jnp.where(ok, (edge_a * TAPS + b) * NBASIS, -PLACES))
    j = lax.broadcasted_iota(jnp.int32, (8, 128), 0)
    _, c = split(lax.broadcasted_iota(jnp.int32, (8, 128), 1), 4)
    inside = ((c >= j) & (c < HALO), c <= j - (8 - HALO))
    far_lane = lax.broadcasted_iota(jnp.int32, (8, 128), 1)

    def moved(row, shift):
        width = row.shape[1]
        return pltpu.roll(jnp.broadcast_to(row, (8, width)), shift % width, 1)[0:1]

    def skewed(row, rows):
        return pltpu.roll(jnp.broadcast_to(row, (rows, row.shape[1])), 0, 1, stride=1, stride_axis=0)

    for k in range(NBASIS):
        put = (place == band_at + k).astype(F32).astype(BF)
        vec = lax.dot_general(rows, put, OVER_ROWS, preferred_element_type=F32)
        edge_vec = []
        for w in range(2):
            put = (edge_place == edge_at[w] + k).astype(F32).astype(BF)
            edge_vec.append(lax.dot_general(rows, put, OVER_ROWS, preferred_element_type=F32))
        for i in range(ROWS):
            own = slice(HALO + i, HALO + i + 1)
            start = (i * NBASIS + k) * COLS
            to = slice(start, start + COLS)
            row = jnp.where((a >= HALO - i) & (a < HALO + ROWS - i), vec[own], 0.0)
            row = jnp.broadcast_to(row, (COLS, BAND))
            row = pltpu.roll(row, (i - HALO) * WIN % BAND, 1, stride=1, stride_axis=0)
            inner_ref[to, :] = row.astype(BF)
            first_rim, at_edge = outer_lanes(i)
            size = outer_rows(i)[1]
            if i < HALO:
                row = jnp.where(a < HALO - i, vec[own], 0.0)[:, :size]
            else:
                row = jnp.where(a >= HALO + ROWS - i, vec[own], 0.0)[:, OUTER:]
                row = moved(row, first_rim + OUTER - (HALO + ROWS - i) * WIN)[:, :size]
            rim = skewed(row, COLS)
            tile = slice(at_edge // 128 * 128, at_edge // 128 * 128 + 128)
            in_edge = (far_lane >= at_edge % 128) & (far_lane < at_edge % 128 + 4 * ROWS)
            for w in range(2):
                row = jnp.where((edge_a >= HALO - i) & (edge_a < HALO + ROWS - i), edge_vec[w][own], 0.0)
                edge = skewed(moved(row, (i - HALO) * 4 + at_edge - 7 * w), 8)
                edge = jnp.where(inside[w] & in_edge, edge, 0.0)
                none = jnp.zeros((8, 128), F32)
                outer_ref[w, to, :size] = rim.astype(BF)
                if w == 0:
                    edge = rim[:EDGE, tile] + jnp.concatenate([edge, none], 0)
                    outer_ref[w, start : start + EDGE, tile] = edge.astype(BF)
                else:
                    edge = rim[COLS - EDGE :, tile] + jnp.concatenate([none, edge], 0)
                    outer_ref[w, start + COLS - EDGE : start + COLS, tile] = edge.astype(BF)


def spread_kernel(info, filt, after, vec_ref):
    lat = my_lat()
    rows = masked_filters(info, filt)
    k, b = split(lax.broadcasted_iota(jnp.int32, (1, SPAN), 1), WIN)
    b = EDGE + HALO - b
    spread_at = jnp.where((b >= 0) & (b < TAPS), b * NBASIS + k, -PLACES)
    place = lax.broadcasted_iota(jnp.int32, (PLACES, SPAN), 0)
    vecs = []
    for a in range(TAPS):
        put = (place == spread_at + a * TAPS * NBASIS).astype(F32).astype(BF)
        vecs.append(lax.dot_general(rows, put, OVER_ROWS, preferred_element_type=F32)[:16])
    e = lax.broadcasted_iota(jnp.int32, (16, SPAN), 0)
    beyond = ((lat == 0) & (e < HALO)) | ((lat == LAT - 1) & (e >= HALO + ROWS))
    for a in range(TAPS):
        vec_ref[a] = jnp.where(beyond, vecs[TAPS - 1 - a], vecs[a])


def each(todo, act):
    for c in todo:
        act(c)


def start_copy(c):
    c.start()


def wait_copy(c):
    c.wait()


def my_core():
    return lax.rem(lax.axis_index("lon"), 2)


def my_lat():
    return lax.axis_index("lat")


def run(todo):
    each(todo, start_copy)
    each(todo, wait_copy)


def row_copies(sources, out, sems, turn):
    todo = []
    for n, (ref, row, columns) in enumerate(sources):
        if turn:
            for m in range(HALO):
                todo.append(pltpu.make_async_copy(ref.at[row + HALO - 1 - m], out.at[m, columns], sems.at[HALO * n + m]))
        else:
            todo.append(pltpu.make_async_copy(ref.at[row : row + HALO], out.at[:, columns], sems.at[HALO * n]))
    return todo


def chip_rows(own, part, out, sems, act):
    for core_is, row, pole in ((0, ROWS - HALO, LAT - 1), (1, 0, 0)):
        half0, half1 = (own, part) if core_is == 0 else (part, own)
        sources = ((half0, row, slice(0, COLS)), (half1, row, slice(COLS, CHIP)))
        for turn in (False, True):

            @pl.when((my_core() == core_is) & ((my_lat() == pole) == turn))
            def _():
                each(row_copies(sources, out, sems, turn), act)


def rows_kernel(own, part, out, sems):
    for core_is, row in ((0, ROWS - HALO), (1, 0)):
        low, high = slice(0, COLS), slice(COLS, CHIP)
        mine, other = (low, high) if core_is == 0 else (high, low)

        @pl.when(my_core() == core_is)
        def _():
            run(row_copies(((own, 0, mine), (part, row, other)), out, sems, False))


def relay_kernel(a_own, e_own, c_own, u_rows, out, u_out, sems):
    del u_rows, u_out
    core, lat = my_core(), my_lat()
    turn = ((core == 0) & (lat == 0)) | ((core == 1) & (lat == LAT - 1))
    todo = [
        pltpu.make_async_copy(e_own, out.at[HALO, 0:PACKED], sems.at[0]),
        pltpu.make_async_copy(c_own, out.at[HALO, COLS : COLS + PACKED], sems.at[1]),
    ]
    each(todo, start_copy)

    @pl.when(turn)
    def _():
        run([pltpu.make_async_copy(a_own.at[HALO - 1 - m], out.at[m], sems.at[2 + m]) for m in range(HALO)])

    @pl.when(jnp.logical_not(turn))
    def _():
        run([pltpu.make_async_copy(a_own, out.at[0:HALO], sems.at[2])])

    each(todo, wait_copy)


PACKED = 3 * EDGE


def gather_columns(rows, firsts):
    slot = lax.broadcasted_iota(jnp.int32, (EDGE, CHANNELS), 0)
    out = jnp.zeros((EDGE, CHANNELS), F32)
    for m, (row, first) in enumerate(zip(rows, firsts)):
        shift = (4 * m - (0 if first else EDGE - HALO)) % EDGE
        moved = pltpu.roll(row.astype(F32), shift, 0)
        out = jnp.where((slot >= 4 * m) & (slot < 4 * m + HALO), moved, out)
    return out.astype(BF)


def pack_columns(out, rows, firsts):
    for g in range(3):
        four = slice(4 * g, 4 * g + 4)
        out[g * EDGE : (g + 1) * EDGE] = gather_columns(rows[four], firsts[four])


def spread_columns(rim, which, row, first):
    at = 2 * HALO * which + row
    block, m = at // 4 - which, at % 4
    slot = lax.broadcasted_iota(jnp.int32, (EDGE, CHANNELS), 0)
    shift = ((0 if first else EDGE - HALO) - 4 * m) % EDGE
    moved = pltpu.roll(rim[block * EDGE : (block + 1) * EDGE].astype(F32), shift, 0)
    keep = slot < HALO if first else slot >= EDGE - HALO
    return jnp.where(keep, moved, 0.0).astype(BF)


def edges_kernel(f_own, f_part, u_own, u_part, edge, corner, outer, sides, sems):
    first, last = slice(0, EDGE), slice(COLS - EDGE, COLS)

    def copies(columns, row, halves):
        todo = []
        for n, (own, half0, half1) in enumerate(halves):
            at = pl.ds(row, HALO)
            todo.append(pltpu.make_async_copy(own.at[:, columns], outer.at[n], sems.at[3 * n]))
            todo.append(pltpu.make_async_copy(half0.at[at, first], sides.at[n, 0], sems.at[3 * n + 1]))
            todo.append(pltpu.make_async_copy(half1.at[at, last], sides.at[n, 1], sems.at[3 * n + 2]))
        return todo

    @pl.when(my_core() == 0)
    def _():
        run(copies(first, ROWS - HALO, ((f_own, f_own, f_part), (u_own, u_own, u_part))))
        pack_columns(edge, [outer[n, r] for n in range(2) for r in range(ROWS)], [True] * (2 * ROWS))

    @pl.when(my_core() == 1)
    def _():
        run(copies(last, 0, ((f_own, f_part, f_own), (u_own, u_part, u_own))))
        pack_columns(edge, [outer[n, r] for n in range(2) for r in range(ROWS)], [False] * (2 * ROWS))

    places = [(n, side, m) for n in range(2) for side in range(2) for m in range(HALO)]
    pack_columns(corner, [sides[at] for at in places], [side == 0 for _, side, _ in places])


def fill_copies(x, rim, sems, which, lat_is, half0, half1, passed0, passed1, rows0, rows1, start, stop):
    todo = []

    def put(ref, columns, at, rows, n):
        low, high = max(at, start), min(at + columns.stop - columns.start, stop)
        if low < high:
            src = ref.at[:, columns.start + low - at : columns.start + high - at]
            todo.append(pltpu.make_async_copy(src, x.at[rows, low - start : high - start], sems.at[n]))

    def put_row(ref, row, columns, at, to, n):
        low, high = max(at, start), min(at + columns.stop - columns.start, stop)
        if low < high:
            src = ref.at[row, columns.start + low - at : columns.start + high - at]
            todo.append(pltpu.make_async_copy(src, x.at[to, low - start : high - start], sems.at[n]))

    whole, first, last = slice(0, COLS), slice(0, EDGE), slice(COLS - EDGE, COLS)
    left, right = 0, EDGE + CHIP
    mid = slice(HALO, HALO + ROWS)
    for n, (ref, at) in enumerate(((passed1, 0), (passed0, 0), (passed0, COLS), (passed1, COLS))):
        at += EDGE * which
        todo.append(pltpu.make_async_copy(ref.at[HALO, at : at + 2 * EDGE], rim.at[n], sems.at[n]))
    put(half0, whole, EDGE, mid, 4)
    put(half1, whole, EDGE + COLS, mid, 5)
    n = 6
    for side, rows in enumerate((rows0, rows1)):
        to = side * (HALO + ROWS)
        if lat_is == side:
            for m in range(HALO):
                own = HALO - 1 - m + side * (ROWS - HALO)
                put_row(half1, own, last, left, to + m, n + 2 * m + 1)
                put_row(half0, own, first, right, to + m, n + 2 * m + 2)
        put(rows.at[0:HALO], slice(0, CHIP), EDGE, slice(to, to + HALO), n)
        n += 7
    return todo


FILL_SEMS = 20


def fill(act, x, rim, sems, which, half, passed, rows):
    core, lat = my_core(), my_lat()
    for core_is in range(2):
        refs = [pair[core_is ^ c] for pair in (half, passed, rows) for c in range(2)]
        start, stop = core_is * COLS, core_is * COLS + WIN
        for lat_is, here in ((0, lat == 0), (1, lat == LAT - 1), (None, (lat > 0) & (lat < LAT - 1))):

            @pl.when((core == core_is) & here)
            def _():
                each(fill_copies(x, rim, sems, which, lat_is, *refs, start, stop), act)


def fill_rim(x, rim, which, left, right):
    lat = my_lat()
    for at, first in ((left, False), (right, True)):
        if at is None:
            continue
        to = slice(at, at + EDGE)
        for r in range(ROWS):
            x[HALO + r, to, :] = spread_columns(rim[int(first)], which, r, first)
        for side, pole in ((0, 0), (1, LAT - 1)):

            @pl.when(lat != pole)
            def _():
                for m in range(HALO):
                    x[side * (HALO + ROWS) + m, to, :] = spread_columns(rim[2 + side], which, m + (0 if first else HALO), first)


def inner_kernel(f_own, f_part, u_own, u_part, band, acc, up_ref, pole_ref, u_rows, x, ud, sems, row_sems):
    core = my_core()
    chip_rows(u_own, u_part, u_rows, row_sems, start_copy)

    def inputs(act):
        for core_is, (f0, f1, u0, u1) in enumerate(((f_own, f_part, u_own, u_part), (f_part, f_own, u_part, u_own))):
            cols = slice(core_is * HALF, (core_is + 1) * HALF)

            @pl.when(core == core_is)
            def _():
                act(pltpu.make_async_copy(f0, x.at[0:ROWS, EDGE : EDGE + COLS], sems.at[0]))
                act(pltpu.make_async_copy(f1, x.at[0:ROWS, EDGE + COLS : EDGE + CHIP], sems.at[1]))
                act(pltpu.make_async_copy(u0.at[:, :, cols], ud.at[0:ROWS], sems.at[2]))
                act(pltpu.make_async_copy(u1.at[:, :, cols], ud.at[ROWS : 2 * ROWS], sems.at[3]))

    inputs(start_copy)
    x[0:ROWS, 0:EDGE, :] = jnp.zeros((ROWS, EDGE, CHANNELS), BF)
    x[0:ROWS, EDGE + CHIP :, :] = jnp.zeros((ROWS, EDGE, CHANNELS), BF)
    x[ROWS:, :, :] = jnp.zeros((2, WIDE, CHANNELS), BF)
    inputs(wait_copy)
    shift = jnp.where(my_lat() == LAT - 1, ROWS - HALO, 0)
    for m in range(HALO):
        row = HALO - 1 - m + shift
        pole_ref[0, m] = x[row, CHIP : CHIP + EDGE, :]
        pole_ref[1, m] = x[row, EDGE : 2 * EDGE, :]
    for w in range(2):
        cells = x[:, w * COLS : w * COLS + WIN].reshape(BAND, CHANNELS)
        for part in range(3):
            to = slice(part * (TALL // 3), (part + 1) * (TALL // 3))
            acc[w, to] = jnp.dot(band[to], cells, preferred_element_type=F32)
    up_ref[...] = ud[...].reshape(2 * CELLS, HALF).T
    chip_rows(u_own, u_part, u_rows, row_sems, wait_copy)


def outer_copies(x, rim, sems, passed0, passed1):
    todo = []
    for n, ref in enumerate((passed0, passed1)):
        todo.append(pltpu.make_async_copy(ref.at[HALO, COLS : COLS + 2 * EDGE], rim.at[n], sems.at[n]))
    low, high = slice(0, WIN - EDGE), slice(CHIP - WIN + EDGE, CHIP)
    n = 2
    for side, rows in enumerate((passed0, passed1)):
        first, block, at = (0, HALO, 0) if side == 0 else (1, 0, WIN - 2 * EDGE)
        to = slice(first, first + HALO)
        todo.append(pltpu.make_async_copy(rows.at[0:HALO, low], x.at[side, 0, to, EDGE:WIN], sems.at[n]))
        todo.append(pltpu.make_async_copy(rows.at[0:HALO, high], x.at[side, 1, to, 0 : WIN - EDGE], sems.at[n + 1]))
        for w, ref in enumerate((passed1, passed0)):
            columns = ref.at[HALO, 0 : 2 * EDGE]
            todo.append(pltpu.make_async_copy(columns, x.at[side, w, block, at : at + 2 * EDGE], sems.at[n + 2 + w]))
        n += 4
    return todo


OUTER_SEMS = 10


def grad_kernel(p_own, p_part, pole_ref, acc, band, up, g_ref, own_ref, x, rim, basis, g, sems):
    core, lat = my_core(), my_lat()

    def inputs(act):
        for core_is, refs in enumerate(((p_own, p_part), (p_part, p_own))):

            @pl.when(core == core_is)
            def _():
                each(outer_copies(x, rim, sems, *refs), act)

    inputs(start_copy)
    for w in range(2):
        x[0, w, HALO, 2 * EDGE :, :] = jnp.zeros((WIN - 2 * EDGE, CHANNELS), BF)
        x[1, w, 0, : WIN - 2 * EDGE, :] = jnp.zeros((WIN - 2 * EDGE, CHANNELS), BF)
    inputs(wait_copy)
    for w, first in ((0, False), (1, True)):
        at = w * (WIN - EDGE)
        for side, pole in ((0, 0), (1, LAT - 1)):

            @pl.when(lat != pole)
            def _():
                for m in range(HALO):
                    x[side, w, side + m, at : at + EDGE, :] = spread_columns(rim[side], 0, m + (0 if first else HALO), first)

            @pl.when(lat == pole)
            def _():
                for m in range(HALO):
                    x[side, w, side + m, at : at + EDGE, :] = pole_ref[w, m]

    for i in range(ROWS):
        to = slice(i * NBASIS * COLS, (i + 1) * NBASIS * COLS)
        first, size = outer_rows(i)
        for w in range(2):
            cells = x[i // HALO, w].reshape(OUTER, CHANNELS)[first : first + size]
            rows = (acc[w, to] + jnp.dot(band[w, to, :size], cells, preferred_element_type=F32)).astype(BF)
            at = w * CELLS + i * COLS
            for k in range(NBASIS):
                basis[k, at : at + COLS, :] = rows[k * COLS : (k + 1) * COLS]
    at = pl.multiple_of(core * CELLS, CELLS)
    own_copy = pltpu.make_async_copy(basis.at[:, pl.ds(at, CELLS)], own_ref, sems.at[4])
    own_copy.start()
    outs = []
    for k in range(NBASIS):
        to = slice(k * CHANNELS, (k + 1) * CHANNELS)
        g[to, :] = jnp.dot(up[...], basis[k], preferred_element_type=F32).astype(BF).T
        outs.append(pltpu.make_async_copy(g.at[to], g_ref.at[to], sems.at[k]))
        outs[-1].start()
    own_copy.wait()
    each(outs, wait_copy)


def tie_kernel(rows, after, out):
    del rows, after, out


def conv_kernel(own_ref, w_ref, conv_ref):
    total = jnp.zeros((CELLS, CHANNELS), F32)
    for k in range(NBASIS):
        total = total + jnp.dot(own_ref[k], w_ref[k * CHANNELS : (k + 1) * CHANNELS, :], preferred_element_type=F32)
    conv_ref[...] = total.astype(BF).reshape(ROWS, COLS, CHANNELS)


def state_kernel(w_ref, vec_ref, u_own, u_part, p_own, p_part, a_own, a_part, state_ref, x, rim, bg, acc, sems):
    def inputs(act):
        fill(act, x, rim, sems, 1, (u_own, u_part), (p_own, p_part), (a_own, a_part))

    inputs(start_copy)
    inputs(wait_copy)

    @pl.when(my_core() == 0)
    def _():
        fill_rim(x, rim, 1, 0, None)

    @pl.when(my_core() == 1)
    def _():
        fill_rim(x, rim, 1, None, WIN - EDGE)

    for k in range(NBASIS):
        wk = w_ref[k * CHANNELS : (k + 1) * CHANNELS, :]
        for part in range(3):
            cells = x[part * 4 : (part + 1) * 4].reshape(4 * WIN, CHANNELS)
            got = lax.dot_general(cells, wk, (((1,), (1,)), ((), ())), preferred_element_type=F32)
            bg[part * 4 : (part + 1) * 4, k * WIN : (k + 1) * WIN, :] = got.astype(BF).reshape(4, WIN, CHANNELS)
    acc[...] = jnp.zeros((ROWS, COLS, CHANNELS), F32)
    for e in range(EXT):
        rows = [r for r in range(ROWS) if 0 <= r + TAPS - 1 - e < TAPS]
        blocks = []
        for r in rows:
            a = r + TAPS - 1 - e
            row = jnp.broadcast_to(vec_ref[a, e : e + 1, :], (COLS, SPAN))
            blocks.append(pltpu.roll(row, 0, 1, stride=1, stride_axis=0).astype(BF))
        got = jnp.dot(jnp.concatenate(blocks, 0), bg[e], preferred_element_type=F32)
        for n, r in enumerate(rows):
            acc[r] += got[n * COLS : (n + 1) * COLS]
    state_ref[...] = acc[...].astype(BF)


def total_kernel(pieces, out):
    for t in range(2):
        out[:, t * HALF : (t + 1) * HALF] = jnp.sum(pieces[:, t].astype(F32), 0)


def on_device(features, upstream, weights, filter_basis, lat_width, lat_offset, lon_reach):
    core = my_core()
    info = jnp.concatenate([lat_width, lat_offset, lon_reach])

    f_part = send(features, to_partner)
    u_part = send(upstream, to_partner)
    own_rows = jnp.where(core == 0, features[ROWS - HALO :], features[:HALO])
    rows = pl.pallas_call(
        rows_kernel,
        out_shape=jax.ShapeDtypeStruct((HALO, CHIP, CHANNELS), BF),
        in_specs=[ANY, ANY],
        out_specs=ANY,
        scratch_shapes=[pltpu.SemaphoreType.DMA((2 * HALO,))],
        compiler_params=params(4),
        cost_estimate=cost(1000, 2_000_000),
        name="rows",
    )(own_rows, f_part)
    af_own = send(rows, along_meridian)
    filt = jnp.transpose(filter_basis, (2, 3, 0, 1)).reshape(PLACES, NLAT)
    inner_band, outer_band = pl.pallas_call(
        bands_kernel,
        out_shape=(
            jax.ShapeDtypeStruct((TALL, BAND), BF),
            jax.ShapeDtypeStruct((2, TALL, OUTER), BF),
        ),
        in_specs=[SMEM, VMEM],
        out_specs=(VMEM, VMEM),
        compiler_params=params(16),
        cost_estimate=cost(2_000_000_000, 5_000_000),
        name="bands",
    )(info, filt)

    edges, corners = pl.pallas_call(
        edges_kernel,
        out_shape=(
            jax.ShapeDtypeStruct((PACKED, CHANNELS), BF),
            jax.ShapeDtypeStruct((PACKED, CHANNELS), BF),
        ),
        in_specs=[ANY] * 4,
        out_specs=(VMEM, VMEM),
        scratch_shapes=[
            pltpu.VMEM((2, ROWS, EDGE, CHANNELS), BF),
            pltpu.VMEM((2, 2, HALO, EDGE, CHANNELS), BF),
            pltpu.SemaphoreType.DMA((6,)),
        ],
        compiler_params=params(4),
        cost_estimate=cost(1000, 1_000_000),
        name="edges",
    )(features, f_part, upstream, u_part)
    e_own = send(edges, to_chip)
    c_own = send(corners, across)
    acc, up, pole, u_rows = pl.pallas_call(
        inner_kernel,
        out_shape=(
            jax.ShapeDtypeStruct((2, TALL, CHANNELS), F32),
            jax.ShapeDtypeStruct((HALF, 2 * CELLS), BF),
            jax.ShapeDtypeStruct((2, HALO, EDGE, CHANNELS), BF),
            jax.ShapeDtypeStruct((HALO, CHIP, CHANNELS), BF),
        ),
        in_specs=[ANY] * 4 + [VMEM],
        out_specs=(VMEM, VMEM, VMEM, ANY),
        scratch_shapes=[
            pltpu.VMEM((ROWS + 2, WIDE, CHANNELS), BF),
            pltpu.VMEM((2 * ROWS, COLS, HALF), BF),
            pltpu.SemaphoreType.DMA((4,)),
            pltpu.SemaphoreType.DMA((2 * HALO,)),
        ],
        compiler_params=params(28),
        cost_estimate=cost(4_000_000_000, 16_000_000),
        name="inner",
    )(features, f_part, upstream, u_part, inner_band)
    passed, u_rows = pl.pallas_call(
        relay_kernel,
        out_shape=(
            jax.ShapeDtypeStruct((HALO + 1, CHIP, CHANNELS), BF),
            jax.ShapeDtypeStruct((HALO, CHIP, CHANNELS), BF),
        ),
        in_specs=[ANY] * 4,
        out_specs=(ANY, ANY),
        input_output_aliases={3: 1},
        scratch_shapes=[pltpu.SemaphoreType.DMA((2 + HALO,))],
        compiler_params=params(4),
        cost_estimate=cost(1000, 4_000_000),
        name="relay",
    )(af_own, e_own, c_own, u_rows)
    p_part = send(passed, to_partner)
    au_own = send(u_rows, along_meridian)
    partial, basis_own = pl.pallas_call(
        grad_kernel,
        out_shape=(
            pltpu.HBM((NBASIS * CHANNELS, HALF), BF),
            pltpu.HBM((NBASIS, CELLS, CHANNELS), BF),
        ),
        in_specs=[ANY] * 2 + [VMEM] * 4,
        out_specs=(HBM, HBM),
        scratch_shapes=[
            pltpu.VMEM((2, 2, 1 + HALO, WIN, CHANNELS), BF),
            pltpu.VMEM((2, 2 * EDGE, CHANNELS), BF),
            pltpu.VMEM((NBASIS, 2 * CELLS, CHANNELS), BF),
            pltpu.VMEM((NBASIS * CHANNELS, HALF), BF),
            pltpu.SemaphoreType.DMA((OUTER_SEMS,)),
        ],
        compiler_params=params(30),
        cost_estimate=cost(6_000_000_000, 12_000_000),
        name="grad",
    )(passed, p_part, pole, acc, outer_band, up)

    pieces = lax.all_to_all(partial.reshape(LAT * LON, OWNED, HALF), BOTH, 0, 0, tiled=True)

    convolved = pl.pallas_call(
        conv_kernel,
        out_shape=jax.ShapeDtypeStruct((ROWS, COLS, CHANNELS), BF),
        in_specs=[VMEM] * 2,
        out_specs=VMEM,
        compiler_params=params(20),
        cost_estimate=cost(80_000_000_000, 8_000_000),
        name="conv",
    )(basis_own, weights)
    au_own = pl.pallas_call(
        tie_kernel,
        out_shape=jax.ShapeDtypeStruct(au_own.shape, BF),
        in_specs=[ANY, ANY],
        out_specs=ANY,
        input_output_aliases={0: 0},
        compiler_params=params(1),
        name="tie",
    )(au_own, in_hbm(convolved))
    au_part = send(au_own, to_partner)
    vecs = pl.pallas_call(
        spread_kernel,
        out_shape=jax.ShapeDtypeStruct((TAPS, 16, SPAN), F32),
        in_specs=[SMEM, VMEM, HBM],
        out_specs=VMEM,
        compiler_params=params(8),
        cost_estimate=cost(1_000_000_000, 1_000_000),
        name="spread",
    )(info, filt, in_hbm(convolved))
    state_grad = pl.pallas_call(
        state_kernel,
        out_shape=jax.ShapeDtypeStruct((ROWS, COLS, CHANNELS), BF),
        in_specs=[VMEM] * 2 + [ANY] * 6,
        out_specs=VMEM,
        scratch_shapes=[
            pltpu.VMEM((EXT, WIN, CHANNELS), BF),
            pltpu.VMEM((4, 2 * EDGE, CHANNELS), BF),
            pltpu.VMEM((EXT, SPAN, CHANNELS), BF),
            pltpu.VMEM((ROWS, COLS, CHANNELS), F32),
            pltpu.SemaphoreType.DMA((FILL_SEMS,)),
        ],
        compiler_params=params(28),
        cost_estimate=cost(8_000_000_000, 12_000_000),
        name="state",
    )(weights, vecs, upstream, u_part, passed, p_part, au_own, au_part)

    weight_grad = pl.pallas_call(
        total_kernel,
        out_shape=jax.ShapeDtypeStruct((OWNED, CHANNELS), F32),
        in_specs=[VMEM],
        out_specs=VMEM,
        compiler_params=params(16),
        name="total",
    )(pltpu.with_memory_space_constraint(pieces.reshape(LAT * LON // 2, 2, OWNED, HALF), pltpu.VMEM))
    return convolved, state_grad, weight_grad


def solution(mesh):
    return jax.shard_map(
        on_device,
        mesh=mesh,
        in_specs=(P("lat", "lon", None), P("lat", "lon", None), P(), P(), P(), P(), P()),
        out_specs=(P("lat", "lon", None), P("lat", "lon", None), P(("lat", "lon"), None)),
        check_vma=False,
    )
```

```python
import jax
import jax.numpy as jnp
from jax import lax
from jax.experimental import pallas as pl
from jax.experimental.pallas import tpu as pltpu
from jax.sharding import PartitionSpec as P

CHANNELS = 768
NBASIS = 4
HALO = 3
TAPS = 7
LAT = 32
LON = 4
NLAT = 192
ROWS = 6
COLS = 64
EDGE = 16
WIN = COLS + 2 * EDGE
CHIP = 2 * COLS
WIDE = CHIP + 2 * EDGE
EXT = ROWS + 2 * HALO
HALF = CHANNELS // 2
CELLS = ROWS * COLS
BAND = (TAPS + 1) * WIN
SPAN = NBASIS * WIN
OUTER = (HALO + 1) * WIN
TALL = ROWS * NBASIS * COLS
PLACES = TAPS * TAPS * NBASIS
OWNED = NBASIS * CHANNELS // (LAT * LON)
BF = jnp.bfloat16
F32 = jnp.float32
BOTH = ("lat", "lon")
DEVICES = [(lat, lon) for lat in range(LAT) for lon in range(LON)]

VMEM = pl.BlockSpec(memory_space=pltpu.VMEM)
SMEM = pl.BlockSpec(memory_space=pltpu.SMEM)
ANY = pl.BlockSpec(memory_space=pl.ANY)
HBM = pl.BlockSpec(memory_space=pltpu.HBM)
MIB = 1024 * 1024


def params(mib):
    return pltpu.CompilerParams(vmem_limit_bytes=mib * MIB)


def in_hbm(block):
    return pltpu.with_memory_space_constraint(block, pltpu.HBM)


def cost(flops, size):
    return pl.CostEstimate(flops=flops, bytes_accessed=size, transcendentals=0)


def send(block, move):
    pairs = []
    for lat, lon in DEVICES:
        to = move(lat, lon)
        if to is not None:
            pairs.append((lat * LON + lon, to[0] * LON + to[1]))
    return lax.ppermute(block, BOTH, pairs)


def to_partner(lat, lon):
    return lat, lon ^ 1


def to_chip(lat, lon):
    return lat, lon ^ 2


def along_meridian(lat, lon):
    if lon % 2 == 0:
        return (lat + 1, lon) if lat + 1 < LAT else (lat, lon ^ 3)
    return (lat - 1, lon) if lat > 0 else (lat, lon ^ 3)


def across(lat, lon):
    to_lat = lat + 1 if lon % 2 == 0 else lat - 1
    return (to_lat, lon ^ 2) if 0 <= to_lat < LAT else None


def split(values, size):
    high = jnp.floor((values.astype(F32) + 0.5) * (1.0 / size)).astype(jnp.int32)
    return high, values - high * size


def outer_rows(i):
    return ((0, 384), (96, 256), (192, 128), (64, 128), (64, 256), (0, 384))[i]


def outer_lanes(i):
    first = outer_rows(i)[0]
    if i < HALO:
        return i * WIN - first, HALO * WIN - first
    return WIN - first, WIN - 2 * EDGE - first


def masked_filters(info, filt):
    lat = my_lat()
    lane = lax.broadcasted_iota(jnp.int32, (1, 128), 1)
    row_of = lat * ROWS + lane - HALO
    row_of = jnp.where(row_of < 0, -1 - row_of, row_of)
    row_of = jnp.where(row_of >= NLAT, 2 * NLAT - 1 - row_of, row_of)
    pick = lax.broadcasted_iota(jnp.int32, (NLAT, 128), 0) == row_of
    rows = jnp.dot(filt[...], pick.astype(F32).astype(BF), preferred_element_type=F32)
    low = jnp.zeros((1, 128), jnp.int32)
    high = jnp.zeros((1, 128), jnp.int32)
    far = jnp.zeros((1, 128), jnp.int32)
    for e in range(EXT):
        row = lat * ROWS + e - HALO
        row = jnp.where(row < 0, -1 - row, row)
        row = jnp.where(row >= NLAT, 2 * NLAT - 1 - row, row)
        width, offset, reach = info[row], info[NLAT + row], info[2 * NLAT + row]
        low = jnp.where(lane == e, offset, low)
        high = jnp.where(lane == e, offset + width, high)
        far = jnp.where(lane == e, reach, far)
    a, rest = split(lax.broadcasted_iota(jnp.int32, (PLACES, 128), 0), TAPS * NBASIS)
    b, _ = split(rest, NBASIS)
    keep = (a >= low) & (a < high) & (jnp.abs(b - HALO) <= far)
    return jnp.where(keep, rows, 0.0).astype(BF)


OVER_ROWS = (((0,), (0,)), ((), ()))


def bands_kernel(info, filt, inner_ref, outer_ref):
    rows = masked_filters(info, filt)
    a, b = split(lax.broadcasted_iota(jnp.int32, (1, BAND), 1), WIN)
    b = b - (EDGE - HALO)
    band_at = jnp.where((a < TAPS) & (b >= 0) & (b < TAPS), (a * TAPS + b) * NBASIS, -PLACES)
    place = lax.broadcasted_iota(jnp.int32, (PLACES, BAND), 0)
    edge_a, edge_c = split(lax.broadcasted_iota(jnp.int32, (1, 128), 1), 4)
    edge_place = lax.broadcasted_iota(jnp.int32, (PLACES, 128), 0)
    edge_at = []
    for w in range(2):
        b = edge_c + w * (HALO + 1)
        ok = (edge_a < TAPS) & (edge_c < HALO)
        edge_at.append(jnp.where(ok, (edge_a * TAPS + b) * NBASIS, -PLACES))
    j = lax.broadcasted_iota(jnp.int32, (8, 128), 0)
    _, c = split(lax.broadcasted_iota(jnp.int32, (8, 128), 1), 4)
    inside = ((c >= j) & (c < HALO), c <= j - (8 - HALO))
    far_lane = lax.broadcasted_iota(jnp.int32, (8, 128), 1)

    def moved(row, shift):
        width = row.shape[1]
        return pltpu.roll(jnp.broadcast_to(row, (8, width)), shift % width, 1)[0:1]

    def skewed(row, rows):
        return pltpu.roll(jnp.broadcast_to(row, (rows, row.shape[1])), 0, 1, stride=1, stride_axis=0)

    for k in range(NBASIS):
        put = (place == band_at + k).astype(F32).astype(BF)
        vec = lax.dot_general(rows, put, OVER_ROWS, preferred_element_type=F32)
        edge_vec = []
        for w in range(2):
            put = (edge_place == edge_at[w] + k).astype(F32).astype(BF)
            edge_vec.append(lax.dot_general(rows, put, OVER_ROWS, preferred_element_type=F32))
        for i in range(ROWS):
            own = slice(HALO + i, HALO + i + 1)
            start = (i * NBASIS + k) * COLS
            to = slice(start, start + COLS)
            row = jnp.where((a >= HALO - i) & (a < HALO + ROWS - i), vec[own], 0.0)
            row = jnp.broadcast_to(row, (COLS, BAND))
            row = pltpu.roll(row, (i - HALO) * WIN % BAND, 1, stride=1, stride_axis=0)
            inner_ref[to, :] = row.astype(BF)
            first_rim, at_edge = outer_lanes(i)
            size = outer_rows(i)[1]
            if i < HALO:
                row = jnp.where(a < HALO - i, vec[own], 0.0)[:, :size]
            else:
                row = jnp.where(a >= HALO + ROWS - i, vec[own], 0.0)[:, OUTER:]
                row = moved(row, first_rim + OUTER - (HALO + ROWS - i) * WIN)[:, :size]
            rim = skewed(row, COLS)
            tile = slice(at_edge // 128 * 128, at_edge // 128 * 128 + 128)
            in_edge = (far_lane >= at_edge % 128) & (far_lane < at_edge % 128 + 4 * ROWS)
            for w in range(2):
                row = jnp.where((edge_a >= HALO - i) & (edge_a < HALO + ROWS - i), edge_vec[w][own], 0.0)
                edge = skewed(moved(row, (i - HALO) * 4 + at_edge - 7 * w), 8)
                edge = jnp.where(inside[w] & in_edge, edge, 0.0)
                none = jnp.zeros((8, 128), F32)
                outer_ref[w, to, :size] = rim.astype(BF)
                if w == 0:
                    edge = rim[:EDGE, tile] + jnp.concatenate([edge, none], 0)
                    outer_ref[w, start : start + EDGE, tile] = edge.astype(BF)
                else:
                    edge = rim[COLS - EDGE :, tile] + jnp.concatenate([none, edge], 0)
                    outer_ref[w, start + COLS - EDGE : start + COLS, tile] = edge.astype(BF)


def spread_kernel(info, filt, after, vec_ref):
    lat = my_lat()
    rows = masked_filters(info, filt)
    k, b = split(lax.broadcasted_iota(jnp.int32, (1, SPAN), 1), WIN)
    b = EDGE + HALO - b
    spread_at = jnp.where((b >= 0) & (b < TAPS), b * NBASIS + k, -PLACES)
    place = lax.broadcasted_iota(jnp.int32, (PLACES, SPAN), 0)
    vecs = []
    for a in range(TAPS):
        put = (place == spread_at + a * TAPS * NBASIS).astype(F32).astype(BF)
        vecs.append(lax.dot_general(rows, put, OVER_ROWS, preferred_element_type=F32)[:16])
    e = lax.broadcasted_iota(jnp.int32, (16, SPAN), 0)
    beyond = ((lat == 0) & (e < HALO)) | ((lat == LAT - 1) & (e >= HALO + ROWS))
    for a in range(TAPS):
        vec_ref[a] = jnp.where(beyond, vecs[TAPS - 1 - a], vecs[a])


def each(todo, act):
    for c in todo:
        act(c)


def start_copy(c):
    c.start()


def wait_copy(c):
    c.wait()


def my_core():
    return lax.rem(lax.axis_index("lon"), 2)


def my_lat():
    return lax.axis_index("lat")


def run(todo):
    each(todo, start_copy)
    each(todo, wait_copy)


def row_copies(sources, out, sems, turn):
    todo = []
    for n, (ref, row, columns) in enumerate(sources):
        if turn:
            for m in range(HALO):
                todo.append(pltpu.make_async_copy(ref.at[row + HALO - 1 - m], out.at[m, columns], sems.at[HALO * n + m]))
        else:
            todo.append(pltpu.make_async_copy(ref.at[row : row + HALO], out.at[:, columns], sems.at[HALO * n]))
    return todo


def chip_rows(own, part, out, sems, act):
    for core_is, row, pole in ((0, ROWS - HALO, LAT - 1), (1, 0, 0)):
        half0, half1 = (own, part) if core_is == 0 else (part, own)
        sources = ((half0, row, slice(0, COLS)), (half1, row, slice(COLS, CHIP)))
        for turn in (False, True):

            @pl.when((my_core() == core_is) & ((my_lat() == pole) == turn))
            def _():
                each(row_copies(sources, out, sems, turn), act)


def rows_kernel(own, part, out, sems):
    for core_is, row in ((0, ROWS - HALO), (1, 0)):
        low, high = slice(0, COLS), slice(COLS, CHIP)
        mine, other = (low, high) if core_is == 0 else (high, low)

        @pl.when(my_core() == core_is)
        def _():
            run(row_copies(((own, 0, mine), (part, row, other)), out, sems, False))


def relay_kernel(a_own, e_own, c_own, u_rows, out, u_out):
    del u_rows, u_out
    core, lat = my_core(), my_lat()
    turn = ((core == 0) & (lat == 0)) | ((core == 1) & (lat == LAT - 1))
    out[HALO, 0:PACKED] = e_own[...]
    out[HALO, COLS : COLS + PACKED] = c_own[...]

    @pl.when(turn)
    def _():
        for m in range(HALO):
            out[m] = a_own[HALO - 1 - m]

    @pl.when(jnp.logical_not(turn))
    def _():
        out[0:HALO] = a_own[...]


PACKED = 3 * EDGE


def gather_columns(rows, firsts):
    slot = lax.broadcasted_iota(jnp.int32, (EDGE, CHANNELS), 0)
    out = jnp.zeros((EDGE, CHANNELS), F32)
    for m, (row, first) in enumerate(zip(rows, firsts)):
        shift = (4 * m - (0 if first else EDGE - HALO)) % EDGE
        moved = pltpu.roll(row.astype(F32), shift, 0)
        out = jnp.where((slot >= 4 * m) & (slot < 4 * m + HALO), moved, out)
    return out.astype(BF)


def pack_columns(out, rows, firsts):
    for g in range(3):
        four = slice(4 * g, 4 * g + 4)
        out[g * EDGE : (g + 1) * EDGE] = gather_columns(rows[four], firsts[four])


def spread_columns(rim, which, row, first):
    at = 2 * HALO * which + row
    block, m = at // 4 - which, at % 4
    slot = lax.broadcasted_iota(jnp.int32, (EDGE, CHANNELS), 0)
    shift = ((0 if first else EDGE - HALO) - 4 * m) % EDGE
    moved = pltpu.roll(rim[block * EDGE : (block + 1) * EDGE].astype(F32), shift, 0)
    keep = slot < HALO if first else slot >= EDGE - HALO
    return jnp.where(keep, moved, 0.0).astype(BF)


def edges_kernel(f_own, f_part, u_own, u_part, edge, corner, outer, sides, sems):
    first, last = slice(0, EDGE), slice(COLS - EDGE, COLS)

    def copies(columns, row, halves):
        todo = []
        for n, (own, half0, half1) in enumerate(halves):
            at = pl.ds(row, HALO)
            todo.append(pltpu.make_async_copy(own.at[:, columns], outer.at[n], sems.at[3 * n]))
            todo.append(pltpu.make_async_copy(half0.at[at, first], sides.at[n, 0], sems.at[3 * n + 1]))
            todo.append(pltpu.make_async_copy(half1.at[at, last], sides.at[n, 1], sems.at[3 * n + 2]))
        return todo

    @pl.when(my_core() == 0)
    def _():
        run(copies(first, ROWS - HALO, ((f_own, f_own, f_part), (u_own, u_own, u_part))))
        pack_columns(edge, [outer[n, r] for n in range(2) for r in range(ROWS)], [True] * (2 * ROWS))

    @pl.when(my_core() == 1)
    def _():
        run(copies(last, 0, ((f_own, f_part, f_own), (u_own, u_part, u_own))))
        pack_columns(edge, [outer[n, r] for n in range(2) for r in range(ROWS)], [False] * (2 * ROWS))

    places = [(n, side, m) for n in range(2) for side in range(2) for m in range(HALO)]
    pack_columns(corner, [sides[at] for at in places], [side == 0 for _, side, _ in places])


def fill_copies(x, rim, sems, which, lat_is, half0, half1, passed0, passed1, rows0, rows1, start, stop):
    todo = []

    def put(ref, columns, at, rows, n):
        low, high = max(at, start), min(at + columns.stop - columns.start, stop)
        if low < high:
            src = ref.at[:, columns.start + low - at : columns.start + high - at]
            todo.append(pltpu.make_async_copy(src, x.at[rows, low - start : high - start], sems.at[n]))

    def put_row(ref, row, columns, at, to, n):
        low, high = max(at, start), min(at + columns.stop - columns.start, stop)
        if low < high:
            src = ref.at[row, columns.start + low - at : columns.start + high - at]
            todo.append(pltpu.make_async_copy(src, x.at[to, low - start : high - start], sems.at[n]))

    whole, first, last = slice(0, COLS), slice(0, EDGE), slice(COLS - EDGE, COLS)
    left, right = 0, EDGE + CHIP
    mid = slice(HALO, HALO + ROWS)
    for n, (ref, at) in enumerate(((passed1, 0), (passed0, 0), (passed0, COLS), (passed1, COLS))):
        at += EDGE * which
        todo.append(pltpu.make_async_copy(ref.at[HALO, at : at + 2 * EDGE], rim.at[n], sems.at[n]))
    put(half0, whole, EDGE, mid, 4)
    put(half1, whole, EDGE + COLS, mid, 5)
    n = 6
    for side, rows in enumerate((rows0, rows1)):
        to = side * (HALO + ROWS)
        if lat_is == side:
            for m in range(HALO):
                own = HALO - 1 - m + side * (ROWS - HALO)
                put_row(half1, own, last, left, to + m, n + 2 * m + 1)
                put_row(half0, own, first, right, to + m, n + 2 * m + 2)
        put(rows.at[0:HALO], slice(0, CHIP), EDGE, slice(to, to + HALO), n)
        n += 7
    return todo


FILL_SEMS = 20


def fill(act, x, rim, sems, which, half, passed, rows):
    core, lat = my_core(), my_lat()
    for core_is in range(2):
        refs = [pair[core_is ^ c] for pair in (half, passed, rows) for c in range(2)]
        start, stop = core_is * COLS, core_is * COLS + WIN
        for lat_is, here in ((0, lat == 0), (1, lat == LAT - 1), (None, (lat > 0) & (lat < LAT - 1))):

            @pl.when((core == core_is) & here)
            def _():
                each(fill_copies(x, rim, sems, which, lat_is, *refs, start, stop), act)


def fill_rim(x, rim, which, left, right):
    lat = my_lat()
    for at, first in ((left, False), (right, True)):
        if at is None:
            continue
        to = slice(at, at + EDGE)
        for r in range(ROWS):
            x[HALO + r, to, :] = spread_columns(rim[int(first)], which, r, first)
        for side, pole in ((0, 0), (1, LAT - 1)):

            @pl.when(lat != pole)
            def _():
                for m in range(HALO):
                    x[side * (HALO + ROWS) + m, to, :] = spread_columns(rim[2 + side], which, m + (0 if first else HALO), first)


def inner_kernel(f_own, f_part, u_own, u_part, band, acc, up_ref, pole_ref, u_rows, x, ud, sems, row_sems):
    core = my_core()
    chip_rows(u_own, u_part, u_rows, row_sems, start_copy)

    def inputs(act):
        for core_is, (f0, f1, u0, u1) in enumerate(((f_own, f_part, u_own, u_part), (f_part, f_own, u_part, u_own))):
            cols = slice(core_is * HALF, (core_is + 1) * HALF)

            @pl.when(core == core_is)
            def _():
                act(pltpu.make_async_copy(f0, x.at[0:ROWS, EDGE : EDGE + COLS], sems.at[0]))
                act(pltpu.make_async_copy(f1, x.at[0:ROWS, EDGE + COLS : EDGE + CHIP], sems.at[1]))
                act(pltpu.make_async_copy(u0.at[:, :, cols], ud.at[0:ROWS], sems.at[2]))
                act(pltpu.make_async_copy(u1.at[:, :, cols], ud.at[ROWS : 2 * ROWS], sems.at[3]))

    inputs(start_copy)
    x[0:ROWS, 0:EDGE, :] = jnp.zeros((ROWS, EDGE, CHANNELS), BF)
    x[0:ROWS, EDGE + CHIP :, :] = jnp.zeros((ROWS, EDGE, CHANNELS), BF)
    x[ROWS:, :, :] = jnp.zeros((2, WIDE, CHANNELS), BF)
    inputs(wait_copy)
    shift = jnp.where(my_lat() == LAT - 1, ROWS - HALO, 0)
    for m in range(HALO):
        row = HALO - 1 - m + shift
        pole_ref[0, m] = x[row, CHIP : CHIP + EDGE, :]
        pole_ref[1, m] = x[row, EDGE : 2 * EDGE, :]
    for w in range(2):
        cells = x[:, w * COLS : w * COLS + WIN].reshape(BAND, CHANNELS)
        for part in range(3):
            to = slice(part * (TALL // 3), (part + 1) * (TALL // 3))
            acc[w, to] = jnp.dot(band[to], cells, preferred_element_type=F32)
    up_ref[...] = ud[...].reshape(2 * CELLS, HALF).T
    chip_rows(u_own, u_part, u_rows, row_sems, wait_copy)


def fill_outer(x, passed0, passed1, pole_ref):
    lat = my_lat()
    low, high = slice(0, WIN - EDGE), slice(CHIP - WIN + EDGE, CHIP)
    for side, (rows, pole) in enumerate(((passed0, 0), (passed1, LAT - 1))):
        block, at, none = (HALO, 0, slice(2 * EDGE, WIN)) if side == 0 else (0, WIN - 2 * EDGE, slice(0, WIN - 2 * EDGE))
        for w, edges in enumerate((passed1, passed0)):
            x[side, w, block, none, :] = jnp.zeros((WIN - 2 * EDGE, CHANNELS), BF)
            x[side, w, block, at : at + 2 * EDGE, :] = edges[HALO, 0 : 2 * EDGE]
            to = slice(EDGE, WIN) if w == 0 else slice(0, WIN - EDGE)
            for m in range(HALO):
                x[side, w, side + m, to, :] = rows[m, low if w == 0 else high]
        corners = rows.at[HALO, COLS : COLS + 2 * EDGE]

        @pl.when(lat != pole)
        def _():
            for w in range(2):
                at = w * (WIN - EDGE)
                for m in range(HALO):
                    x[side, w, side + m, at : at + EDGE, :] = spread_columns(corners, 0, m + (HALO if w == 0 else 0), w == 1)

        @pl.when(lat == pole)
        def _():
            for w in range(2):
                at = w * (WIN - EDGE)
                for m in range(HALO):
                    x[side, w, side + m, at : at + EDGE, :] = pole_ref[w, m]


def grad_kernel(p_own, p_part, pole_ref, acc, band, up, g_ref, own_ref, x, basis, g, sems):
    core = my_core()

    @pl.when(core == 0)
    def _():
        fill_outer(x, p_own, p_part, pole_ref)

    @pl.when(core == 1)
    def _():
        fill_outer(x, p_part, p_own, pole_ref)

    for i in range(ROWS):
        to = slice(i * NBASIS * COLS, (i + 1) * NBASIS * COLS)
        first, size = outer_rows(i)
        for w in range(2):
            cells = x[i // HALO, w].reshape(OUTER, CHANNELS)[first : first + size]
            rows = (acc[w, to] + jnp.dot(band[w, to, :size], cells, preferred_element_type=F32)).astype(BF)
            at = w * CELLS + i * COLS
            for k in range(NBASIS):
                basis[k, at : at + COLS, :] = rows[k * COLS : (k + 1) * COLS]
    at = pl.multiple_of(core * CELLS, CELLS)
    own_copy = pltpu.make_async_copy(basis.at[:, pl.ds(at, CELLS)], own_ref, sems.at[4])
    own_copy.start()
    outs = []
    for k in range(NBASIS):
        to = slice(k * CHANNELS, (k + 1) * CHANNELS)
        g[to, :] = jnp.dot(up[...], basis[k], preferred_element_type=F32).astype(BF).T
        outs.append(pltpu.make_async_copy(g.at[to], g_ref.at[to], sems.at[k]))
        outs[-1].start()
    own_copy.wait()
    each(outs, wait_copy)


def tie_kernel(rows, after, out):
    del rows, after, out


def conv_kernel(own_ref, w_ref, conv_ref):
    total = jnp.zeros((CELLS, CHANNELS), F32)
    for k in range(NBASIS):
        total = total + jnp.dot(own_ref[k], w_ref[k * CHANNELS : (k + 1) * CHANNELS, :], preferred_element_type=F32)
    conv_ref[...] = total.astype(BF).reshape(ROWS, COLS, CHANNELS)


def state_kernel(w_ref, vec_ref, u_own, u_part, p_own, p_part, a_own, a_part, state_ref, x, rim, bg, acc, sems):
    def inputs(act):
        fill(act, x, rim, sems, 1, (u_own, u_part), (p_own, p_part), (a_own, a_part))

    inputs(start_copy)
    inputs(wait_copy)

    @pl.when(my_core() == 0)
    def _():
        fill_rim(x, rim, 1, 0, None)

    @pl.when(my_core() == 1)
    def _():
        fill_rim(x, rim, 1, None, WIN - EDGE)

    for k in range(NBASIS):
        wk = w_ref[k * CHANNELS : (k + 1) * CHANNELS, :]
        for part in range(3):
            cells = x[part * 4 : (part + 1) * 4].reshape(4 * WIN, CHANNELS)
            got = lax.dot_general(cells, wk, (((1,), (1,)), ((), ())), preferred_element_type=F32)
            bg[part * 4 : (part + 1) * 4, k * WIN : (k + 1) * WIN, :] = got.astype(BF).reshape(4, WIN, CHANNELS)
    acc[...] = jnp.zeros((ROWS, COLS, CHANNELS), F32)
    for e in range(EXT):
        rows = [r for r in range(ROWS) if 0 <= r + TAPS - 1 - e < TAPS]
        blocks = []
        for r in rows:
            a = r + TAPS - 1 - e
            row = jnp.broadcast_to(vec_ref[a, e : e + 1, :], (COLS, SPAN))
            blocks.append(pltpu.roll(row, 0, 1, stride=1, stride_axis=0).astype(BF))
        got = jnp.dot(jnp.concatenate(blocks, 0), bg[e], preferred_element_type=F32)
        for n, r in enumerate(rows):
            acc[r] += got[n * COLS : (n + 1) * COLS]
    state_ref[...] = acc[...].astype(BF)


def total_kernel(pieces, out):
    for t in range(2):
        out[:, t * HALF : (t + 1) * HALF] = jnp.sum(pieces[:, t].astype(F32), 0)


def on_device(features, upstream, weights, filter_basis, lat_width, lat_offset, lon_reach):
    core = my_core()
    info = jnp.concatenate([lat_width, lat_offset, lon_reach])

    f_part = send(features, to_partner)
    u_part = send(upstream, to_partner)
    own_rows = jnp.where(core == 0, features[ROWS - HALO :], features[:HALO])
    rows = pl.pallas_call(
        rows_kernel,
        out_shape=jax.ShapeDtypeStruct((HALO, CHIP, CHANNELS), BF),
        in_specs=[ANY, ANY],
        out_specs=ANY,
        scratch_shapes=[pltpu.SemaphoreType.DMA((2 * HALO,))],
        compiler_params=params(4),
        cost_estimate=cost(1000, 2_000_000),
        name="rows",
    )(own_rows, f_part)
    af_own = send(rows, along_meridian)
    filt = jnp.transpose(filter_basis, (2, 3, 0, 1)).reshape(PLACES, NLAT)
    inner_band, outer_band = pl.pallas_call(
        bands_kernel,
        out_shape=(
            jax.ShapeDtypeStruct((TALL, BAND), BF),
            jax.ShapeDtypeStruct((2, TALL, OUTER), BF),
        ),
        in_specs=[SMEM, VMEM],
        out_specs=(VMEM, VMEM),
        compiler_params=params(16),
        cost_estimate=cost(2_000_000_000, 5_000_000),
        name="bands",
    )(info, filt)

    edges, corners = pl.pallas_call(
        edges_kernel,
        out_shape=(
            jax.ShapeDtypeStruct((PACKED, CHANNELS), BF),
            jax.ShapeDtypeStruct((PACKED, CHANNELS), BF),
        ),
        in_specs=[ANY] * 4,
        out_specs=(VMEM, VMEM),
        scratch_shapes=[
            pltpu.VMEM((2, ROWS, EDGE, CHANNELS), BF),
            pltpu.VMEM((2, 2, HALO, EDGE, CHANNELS), BF),
            pltpu.SemaphoreType.DMA((6,)),
        ],
        compiler_params=params(4),
        cost_estimate=cost(1000, 1_000_000),
        name="edges",
    )(features, f_part, upstream, u_part)
    e_own = send(edges, to_chip)
    c_own = send(corners, across)
    acc, up, pole, u_rows = pl.pallas_call(
        inner_kernel,
        out_shape=(
            jax.ShapeDtypeStruct((2, TALL, CHANNELS), F32),
            jax.ShapeDtypeStruct((HALF, 2 * CELLS), BF),
            jax.ShapeDtypeStruct((2, HALO, EDGE, CHANNELS), BF),
            jax.ShapeDtypeStruct((HALO, CHIP, CHANNELS), BF),
        ),
        in_specs=[ANY] * 4 + [VMEM],
        out_specs=(VMEM, VMEM, VMEM, ANY),
        scratch_shapes=[
            pltpu.VMEM((ROWS + 2, WIDE, CHANNELS), BF),
            pltpu.VMEM((2 * ROWS, COLS, HALF), BF),
            pltpu.SemaphoreType.DMA((4,)),
            pltpu.SemaphoreType.DMA((2 * HALO,)),
        ],
        compiler_params=params(28),
        cost_estimate=cost(4_000_000_000, 16_000_000),
        name="inner",
    )(features, f_part, upstream, u_part, inner_band)
    passed, u_rows = pl.pallas_call(
        relay_kernel,
        out_shape=(
            jax.ShapeDtypeStruct((HALO + 1, CHIP, CHANNELS), BF),
            jax.ShapeDtypeStruct((HALO, CHIP, CHANNELS), BF),
        ),
        in_specs=[VMEM] * 3 + [ANY],
        out_specs=(VMEM, ANY),
        input_output_aliases={3: 1},
        compiler_params=params(8),
        cost_estimate=cost(1000, 4_000_000),
        name="relay",
    )(af_own, e_own, c_own, u_rows)
    p_part = send(passed, to_partner)
    au_own = send(u_rows, along_meridian)
    partial, basis_own = pl.pallas_call(
        grad_kernel,
        out_shape=(
            pltpu.HBM((NBASIS * CHANNELS, HALF), BF),
            pltpu.HBM((NBASIS, CELLS, CHANNELS), BF),
        ),
        in_specs=[VMEM] * 6,
        out_specs=(HBM, HBM),
        scratch_shapes=[
            pltpu.VMEM((2, 2, 1 + HALO, WIN, CHANNELS), BF),
            pltpu.VMEM((NBASIS, 2 * CELLS, CHANNELS), BF),
            pltpu.VMEM((NBASIS * CHANNELS, HALF), BF),
            pltpu.SemaphoreType.DMA((5,)),
        ],
        compiler_params=params(30),
        cost_estimate=cost(6_000_000_000, 12_000_000),
        name="grad",
    )(passed, p_part, pole, acc, outer_band, up)

    pieces = lax.all_to_all(partial.reshape(LAT * LON, OWNED, HALF), BOTH, 0, 0, tiled=True)

    convolved = pl.pallas_call(
        conv_kernel,
        out_shape=jax.ShapeDtypeStruct((ROWS, COLS, CHANNELS), BF),
        in_specs=[VMEM] * 2,
        out_specs=VMEM,
        compiler_params=params(20),
        cost_estimate=cost(80_000_000_000, 8_000_000),
        name="conv",
    )(basis_own, weights)
    au_own = pl.pallas_call(
        tie_kernel,
        out_shape=jax.ShapeDtypeStruct(au_own.shape, BF),
        in_specs=[ANY, ANY],
        out_specs=ANY,
        input_output_aliases={0: 0},
        compiler_params=params(1),
        name="tie",
    )(au_own, in_hbm(convolved))
    au_part = send(au_own, to_partner)
    vecs = pl.pallas_call(
        spread_kernel,
        out_shape=jax.ShapeDtypeStruct((TAPS, 16, SPAN), F32),
        in_specs=[SMEM, VMEM, HBM],
        out_specs=VMEM,
        compiler_params=params(8),
        cost_estimate=cost(1_000_000_000, 1_000_000),
        name="spread",
    )(info, filt, in_hbm(convolved))
    state_grad = pl.pallas_call(
        state_kernel,
        out_shape=jax.ShapeDtypeStruct((ROWS, COLS, CHANNELS), BF),
        in_specs=[VMEM] * 2 + [ANY] * 6,
        out_specs=VMEM,
        scratch_shapes=[
            pltpu.VMEM((EXT, WIN, CHANNELS), BF),
            pltpu.VMEM((4, 2 * EDGE, CHANNELS), BF),
            pltpu.VMEM((EXT, SPAN, CHANNELS), BF),
            pltpu.VMEM((ROWS, COLS, CHANNELS), F32),
            pltpu.SemaphoreType.DMA((FILL_SEMS,)),
        ],
        compiler_params=params(28),
        cost_estimate=cost(8_000_000_000, 12_000_000),
        name="state",
    )(weights, vecs, upstream, u_part, passed, p_part, au_own, au_part)

    weight_grad = pl.pallas_call(
        total_kernel,
        out_shape=jax.ShapeDtypeStruct((OWNED, CHANNELS), F32),
        in_specs=[VMEM],
        out_specs=VMEM,
        compiler_params=params(16),
        name="total",
    )(pltpu.with_memory_space_constraint(pieces.reshape(LAT * LON // 2, 2, OWNED, HALF), pltpu.VMEM))
    return convolved, state_grad, weight_grad


def solution(mesh):
    return jax.shard_map(
        on_device,
        mesh=mesh,
        in_specs=(P("lat", "lon", None), P("lat", "lon", None), P(), P(), P(), P(), P()),
        out_specs=(P("lat", "lon", None), P("lat", "lon", None), P(("lat", "lon"), None)),
        check_vma=False,
    )
```

```python
import jax
import jax.numpy as jnp
from jax import lax
from jax.experimental import pallas as pl
from jax.experimental.pallas import tpu as pltpu
from jax.sharding import PartitionSpec as P

CHANNELS = 768
NBASIS = 4
HALO = 3
TAPS = 7
LAT = 32
LON = 4
NLAT = 192
ROWS = 6
COLS = 64
EDGE = 16
WIN = COLS + 2 * EDGE
CHIP = 2 * COLS
WIDE = CHIP + 2 * EDGE
EXT = ROWS + 2 * HALO
HALF = CHANNELS // 2
CELLS = ROWS * COLS
BAND = (TAPS + 1) * WIN
SPAN = NBASIS * WIN
OUTER = (HALO + 1) * WIN
TALL = ROWS * NBASIS * COLS
PLACES = TAPS * TAPS * NBASIS
OWNED = NBASIS * CHANNELS // (LAT * LON)
BF = jnp.bfloat16
F32 = jnp.float32
BOTH = ("lat", "lon")
DEVICES = [(lat, lon) for lat in range(LAT) for lon in range(LON)]

VMEM = pl.BlockSpec(memory_space=pltpu.VMEM)
SMEM = pl.BlockSpec(memory_space=pltpu.SMEM)
ANY = pl.BlockSpec(memory_space=pl.ANY)
HBM = pl.BlockSpec(memory_space=pltpu.HBM)
MIB = 1024 * 1024


def params(mib):
    return pltpu.CompilerParams(vmem_limit_bytes=mib * MIB)


def in_hbm(block):
    return pltpu.with_memory_space_constraint(block, pltpu.HBM)


def cost(flops, size):
    return pl.CostEstimate(flops=flops, bytes_accessed=size, transcendentals=0)


def send(block, move):
    pairs = []
    for lat, lon in DEVICES:
        to = move(lat, lon)
        if to is not None:
            pairs.append((lat * LON + lon, to[0] * LON + to[1]))
    return lax.ppermute(block, BOTH, pairs)


def to_partner(lat, lon):
    return lat, lon ^ 1


def to_chip(lat, lon):
    return lat, lon ^ 2


def along_meridian(lat, lon):
    if lon % 2 == 0:
        return (lat + 1, lon) if lat + 1 < LAT else (lat, lon ^ 3)
    return (lat - 1, lon) if lat > 0 else (lat, lon ^ 3)


def across(lat, lon):
    to_lat = lat + 1 if lon % 2 == 0 else lat - 1
    return (to_lat, lon ^ 2) if 0 <= to_lat < LAT else None


def split(values, size):
    high = jnp.floor((values.astype(F32) + 0.5) * (1.0 / size)).astype(jnp.int32)
    return high, values - high * size


def outer_rows(i):
    return ((0, 384), (96, 256), (192, 128), (64, 128), (64, 256), (0, 384))[i]


def outer_lanes(i):
    first = outer_rows(i)[0]
    if i < HALO:
        return i * WIN - first, HALO * WIN - first
    return WIN - first, WIN - 2 * EDGE - first


def masked_filters(info, filt):
    lat = my_lat()
    lane = lax.broadcasted_iota(jnp.int32, (1, 128), 1)
    row_of = lat * ROWS + lane - HALO
    row_of = jnp.where(row_of < 0, -1 - row_of, row_of)
    row_of = jnp.where(row_of >= NLAT, 2 * NLAT - 1 - row_of, row_of)
    pick = lax.broadcasted_iota(jnp.int32, (NLAT, 128), 0) == row_of
    rows = jnp.dot(filt[...], pick.astype(F32).astype(BF), preferred_element_type=F32)
    low = jnp.zeros((1, 128), jnp.int32)
    high = jnp.zeros((1, 128), jnp.int32)
    far = jnp.zeros((1, 128), jnp.int32)
    for e in range(EXT):
        row = lat * ROWS + e - HALO
        row = jnp.where(row < 0, -1 - row, row)
        row = jnp.where(row >= NLAT, 2 * NLAT - 1 - row, row)
        width, offset, reach = info[row], info[NLAT + row], info[2 * NLAT + row]
        low = jnp.where(lane == e, offset, low)
        high = jnp.where(lane == e, offset + width, high)
        far = jnp.where(lane == e, reach, far)
    a, rest = split(lax.broadcasted_iota(jnp.int32, (PLACES, 128), 0), TAPS * NBASIS)
    b, _ = split(rest, NBASIS)
    keep = (a >= low) & (a < high) & (jnp.abs(b - HALO) <= far)
    return jnp.where(keep, rows, 0.0).astype(BF)


OVER_ROWS = (((0,), (0,)), ((), ()))


def bands_kernel(info, filt, inner_ref, outer_ref):
    rows = masked_filters(info, filt)
    a, b = split(lax.broadcasted_iota(jnp.int32, (1, BAND), 1), WIN)
    b = b - (EDGE - HALO)
    band_at = jnp.where((a < TAPS) & (b >= 0) & (b < TAPS), (a * TAPS + b) * NBASIS, -PLACES)
    place = lax.broadcasted_iota(jnp.int32, (PLACES, BAND), 0)
    edge_a, edge_c = split(lax.broadcasted_iota(jnp.int32, (1, 128), 1), 4)
    edge_place = lax.broadcasted_iota(jnp.int32, (PLACES, 128), 0)
    edge_at = []
    for w in range(2):
        b = edge_c + w * (HALO + 1)
        ok = (edge_a < TAPS) & (edge_c < HALO)
        edge_at.append(jnp.where(ok, (edge_a * TAPS + b) * NBASIS, -PLACES))
    j = lax.broadcasted_iota(jnp.int32, (8, 128), 0)
    _, c = split(lax.broadcasted_iota(jnp.int32, (8, 128), 1), 4)
    inside = ((c >= j) & (c < HALO), c <= j - (8 - HALO))
    far_lane = lax.broadcasted_iota(jnp.int32, (8, 128), 1)

    def moved(row, shift):
        width = row.shape[1]
        return pltpu.roll(jnp.broadcast_to(row, (8, width)), shift % width, 1)[0:1]

    def skewed(row, rows):
        return pltpu.roll(jnp.broadcast_to(row, (rows, row.shape[1])), 0, 1, stride=1, stride_axis=0)

    for k in range(NBASIS):
        put = (place == band_at + k).astype(F32).astype(BF)
        vec = lax.dot_general(rows, put, OVER_ROWS, preferred_element_type=F32)
        edge_vec = []
        for w in range(2):
            put = (edge_place == edge_at[w] + k).astype(F32).astype(BF)
            edge_vec.append(lax.dot_general(rows, put, OVER_ROWS, preferred_element_type=F32))
        for i in range(ROWS):
            own = slice(HALO + i, HALO + i + 1)
            start = (i * NBASIS + k) * COLS
            to = slice(start, start + COLS)
            row = jnp.where((a >= HALO - i) & (a < HALO + ROWS - i), vec[own], 0.0)
            row = jnp.broadcast_to(row, (COLS, BAND))
            row = pltpu.roll(row, (i - HALO) * WIN % BAND, 1, stride=1, stride_axis=0)
            inner_ref[to, :] = row.astype(BF)
            first_rim, at_edge = outer_lanes(i)
            size = outer_rows(i)[1]
            if i < HALO:
                row = jnp.where(a < HALO - i, vec[own], 0.0)[:, :size]
            else:
                row = jnp.where(a >= HALO + ROWS - i, vec[own], 0.0)[:, OUTER:]
                row = moved(row, first_rim + OUTER - (HALO + ROWS - i) * WIN)[:, :size]
            rim = skewed(row, COLS)
            tile = slice(at_edge // 128 * 128, at_edge // 128 * 128 + 128)
            in_edge = (far_lane >= at_edge % 128) & (far_lane < at_edge % 128 + 4 * ROWS)
            for w in range(2):
                row = jnp.where((edge_a >= HALO - i) & (edge_a < HALO + ROWS - i), edge_vec[w][own], 0.0)
                edge = skewed(moved(row, (i - HALO) * 4 + at_edge - 7 * w), 8)
                edge = jnp.where(inside[w] & in_edge, edge, 0.0)
                none = jnp.zeros((8, 128), F32)
                outer_ref[w, to, :size] = rim.astype(BF)
                if w == 0:
                    edge = rim[:EDGE, tile] + jnp.concatenate([edge, none], 0)
                    outer_ref[w, start : start + EDGE, tile] = edge.astype(BF)
                else:
                    edge = rim[COLS - EDGE :, tile] + jnp.concatenate([none, edge], 0)
                    outer_ref[w, start + COLS - EDGE : start + COLS, tile] = edge.astype(BF)


def spread_kernel(info, filt, after, vec_ref):
    lat = my_lat()
    rows = masked_filters(info, filt)
    k, b = split(lax.broadcasted_iota(jnp.int32, (1, SPAN), 1), WIN)
    b = EDGE + HALO - b
    spread_at = jnp.where((b >= 0) & (b < TAPS), b * NBASIS + k, -PLACES)
    place = lax.broadcasted_iota(jnp.int32, (PLACES, SPAN), 0)
    vecs = []
    for a in range(TAPS):
        put = (place == spread_at + a * TAPS * NBASIS).astype(F32).astype(BF)
        vecs.append(lax.dot_general(rows, put, OVER_ROWS, preferred_element_type=F32)[:16])
    e = lax.broadcasted_iota(jnp.int32, (16, SPAN), 0)
    beyond = ((lat == 0) & (e < HALO)) | ((lat == LAT - 1) & (e >= HALO + ROWS))
    for a in range(TAPS):
        vec_ref[a] = jnp.where(beyond, vecs[TAPS - 1 - a], vecs[a])


def each(todo, act):
    for c in todo:
        act(c)


def start_copy(c):
    c.start()


def wait_copy(c):
    c.wait()


def my_core():
    return lax.rem(lax.axis_index("lon"), 2)


def my_lat():
    return lax.axis_index("lat")


def run(todo):
    each(todo, start_copy)
    each(todo, wait_copy)


def row_copies(sources, out, sems, turn):
    todo = []
    for n, (ref, row, columns) in enumerate(sources):
        if turn:
            for m in range(HALO):
                todo.append(pltpu.make_async_copy(ref.at[row + HALO - 1 - m], out.at[m, columns], sems.at[HALO * n + m]))
        else:
            todo.append(pltpu.make_async_copy(ref.at[row : row + HALO], out.at[:, columns], sems.at[HALO * n]))
    return todo


def chip_rows(own, part, out, sems, act):
    for core_is, row, pole in ((0, ROWS - HALO, LAT - 1), (1, 0, 0)):
        half0, half1 = (own, part) if core_is == 0 else (part, own)
        sources = ((half0, row, slice(0, COLS)), (half1, row, slice(COLS, CHIP)))
        for turn in (False, True):

            @pl.when((my_core() == core_is) & ((my_lat() == pole) == turn))
            def _():
                each(row_copies(sources, out, sems, turn), act)


def rows_kernel(own, part, out, sems):
    for core_is, row in ((0, ROWS - HALO), (1, 0)):
        low, high = slice(0, COLS), slice(COLS, CHIP)
        mine, other = (low, high) if core_is == 0 else (high, low)

        @pl.when(my_core() == core_is)
        def _():
            run(row_copies(((own, 0, mine), (part, row, other)), out, sems, False))


def join_kernel(e_own, c_own, after, out):
    del after
    out[0:PACKED] = e_own[...]
    out[COLS : COLS + PACKED] = c_own[...]


def relay_kernel(a_own, u_rows, after, out, u_out):
    del u_rows, after, u_out
    core, lat = my_core(), my_lat()
    turn = ((core == 0) & (lat == 0)) | ((core == 1) & (lat == LAT - 1))

    @pl.when(turn)
    def _():
        for m in range(HALO):
            out[m] = a_own[HALO - 1 - m]

    @pl.when(jnp.logical_not(turn))
    def _():
        out[...] = a_own[...]


PACKED = 3 * EDGE


def gather_columns(rows, firsts):
    slot = lax.broadcasted_iota(jnp.int32, (EDGE, CHANNELS), 0)
    out = jnp.zeros((EDGE, CHANNELS), F32)
    for m, (row, first) in enumerate(zip(rows, firsts)):
        shift = (4 * m - (0 if first else EDGE - HALO)) % EDGE
        moved = pltpu.roll(row.astype(F32), shift, 0)
        out = jnp.where((slot >= 4 * m) & (slot < 4 * m + HALO), moved, out)
    return out.astype(BF)


def pack_columns(out, rows, firsts):
    for g in range(3):
        four = slice(4 * g, 4 * g + 4)
        out[g * EDGE : (g + 1) * EDGE] = gather_columns(rows[four], firsts[four])


def spread_columns(rim, which, row, first):
    at = 2 * HALO * which + row
    block, m = at // 4 - which, at % 4
    slot = lax.broadcasted_iota(jnp.int32, (EDGE, CHANNELS), 0)
    shift = ((0 if first else EDGE - HALO) - 4 * m) % EDGE
    moved = pltpu.roll(rim[block * EDGE : (block + 1) * EDGE].astype(F32), shift, 0)
    keep = slot < HALO if first else slot >= EDGE - HALO
    return jnp.where(keep, moved, 0.0).astype(BF)


def edges_kernel(f_own, f_part, u_own, u_part, edge, corner, outer, sides, sems):
    first, last = slice(0, EDGE), slice(COLS - EDGE, COLS)

    def copies(columns, row, halves):
        todo = []
        for n, (own, half0, half1) in enumerate(halves):
            at = pl.ds(row, HALO)
            todo.append(pltpu.make_async_copy(own.at[:, columns], outer.at[n], sems.at[3 * n]))
            todo.append(pltpu.make_async_copy(half0.at[at, first], sides.at[n, 0], sems.at[3 * n + 1]))
            todo.append(pltpu.make_async_copy(half1.at[at, last], sides.at[n, 1], sems.at[3 * n + 2]))
        return todo

    @pl.when(my_core() == 0)
    def _():
        run(copies(first, ROWS - HALO, ((f_own, f_own, f_part), (u_own, u_own, u_part))))
        pack_columns(edge, [outer[n, r] for n in range(2) for r in range(ROWS)], [True] * (2 * ROWS))

    @pl.when(my_core() == 1)
    def _():
        run(copies(last, 0, ((f_own, f_part, f_own), (u_own, u_part, u_own))))
        pack_columns(edge, [outer[n, r] for n in range(2) for r in range(ROWS)], [False] * (2 * ROWS))

    places = [(n, side, m) for n in range(2) for side in range(2) for m in range(HALO)]
    pack_columns(corner, [sides[at] for at in places], [side == 0 for _, side, _ in places])


def fill_copies(x, rim, sems, which, lat_is, half0, half1, passed0, passed1, rows0, rows1, start, stop):
    todo = []

    def put(ref, columns, at, rows, n):
        low, high = max(at, start), min(at + columns.stop - columns.start, stop)
        if low < high:
            src = ref.at[:, columns.start + low - at : columns.start + high - at]
            todo.append(pltpu.make_async_copy(src, x.at[rows, low - start : high - start], sems.at[n]))

    def put_row(ref, row, columns, at, to, n):
        low, high = max(at, start), min(at + columns.stop - columns.start, stop)
        if low < high:
            src = ref.at[row, columns.start + low - at : columns.start + high - at]
            todo.append(pltpu.make_async_copy(src, x.at[to, low - start : high - start], sems.at[n]))

    whole, first, last = slice(0, COLS), slice(0, EDGE), slice(COLS - EDGE, COLS)
    left, right = 0, EDGE + CHIP
    mid = slice(HALO, HALO + ROWS)
    for n, (ref, at) in enumerate(((passed1, 0), (passed0, 0), (passed0, COLS), (passed1, COLS))):
        at += EDGE * which
        todo.append(pltpu.make_async_copy(ref.at[at : at + 2 * EDGE], rim.at[n], sems.at[n]))
    put(half0, whole, EDGE, mid, 4)
    put(half1, whole, EDGE + COLS, mid, 5)
    n = 6
    for side, rows in enumerate((rows0, rows1)):
        to = side * (HALO + ROWS)
        if lat_is == side:
            for m in range(HALO):
                own = HALO - 1 - m + side * (ROWS - HALO)
                put_row(half1, own, last, left, to + m, n + 2 * m + 1)
                put_row(half0, own, first, right, to + m, n + 2 * m + 2)
        put(rows.at[0:HALO], slice(0, CHIP), EDGE, slice(to, to + HALO), n)
        n += 7
    return todo


FILL_SEMS = 20


def fill(act, x, rim, sems, which, half, passed, rows):
    core, lat = my_core(), my_lat()
    for core_is in range(2):
        refs = [pair[core_is ^ c] for pair in (half, passed, rows) for c in range(2)]
        start, stop = core_is * COLS, core_is * COLS + WIN
        for lat_is, here in ((0, lat == 0), (1, lat == LAT - 1), (None, (lat > 0) & (lat < LAT - 1))):

            @pl.when((core == core_is) & here)
            def _():
                each(fill_copies(x, rim, sems, which, lat_is, *refs, start, stop), act)


def fill_rim(x, rim, which, left, right):
    lat = my_lat()
    for at, first in ((left, False), (right, True)):
        if at is None:
            continue
        to = slice(at, at + EDGE)
        for r in range(ROWS):
            x[HALO + r, to, :] = spread_columns(rim[int(first)], which, r, first)
        for side, pole in ((0, 0), (1, LAT - 1)):

            @pl.when(lat != pole)
            def _():
                for m in range(HALO):
                    x[side * (HALO + ROWS) + m, to, :] = spread_columns(rim[2 + side], which, m + (0 if first else HALO), first)


def inner_kernel(f_own, f_part, u_own, u_part, band, acc, up_ref, pole_ref, u_rows, x, ud, sems, row_sems):
    core = my_core()
    chip_rows(u_own, u_part, u_rows, row_sems, start_copy)

    def inputs(act):
        for core_is, (f0, f1, u0, u1) in enumerate(((f_own, f_part, u_own, u_part), (f_part, f_own, u_part, u_own))):
            cols = slice(core_is * HALF, (core_is + 1) * HALF)

            @pl.when(core == core_is)
            def _():
                act(pltpu.make_async_copy(f0, x.at[0:ROWS, EDGE : EDGE + COLS], sems.at[0]))
                act(pltpu.make_async_copy(f1, x.at[0:ROWS, EDGE + COLS : EDGE + CHIP], sems.at[1]))
                act(pltpu.make_async_copy(u0.at[:, :, cols], ud.at[0:ROWS], sems.at[2]))
                act(pltpu.make_async_copy(u1.at[:, :, cols], ud.at[ROWS : 2 * ROWS], sems.at[3]))

    inputs(start_copy)
    x[0:ROWS, 0:EDGE, :] = jnp.zeros((ROWS, EDGE, CHANNELS), BF)
    x[0:ROWS, EDGE + CHIP :, :] = jnp.zeros((ROWS, EDGE, CHANNELS), BF)
    x[ROWS:, :, :] = jnp.zeros((2, WIDE, CHANNELS), BF)
    inputs(wait_copy)
    shift = jnp.where(my_lat() == LAT - 1, ROWS - HALO, 0)
    for m in range(HALO):
        row = HALO - 1 - m + shift
        pole_ref[0, m] = x[row, CHIP : CHIP + EDGE, :]
        pole_ref[1, m] = x[row, EDGE : 2 * EDGE, :]
    for w in range(2):
        cells = x[:, w * COLS : w * COLS + WIN].reshape(BAND, CHANNELS)
        for part in range(3):
            to = slice(part * (TALL // 3), (part + 1) * (TALL // 3))
            acc[w, to] = jnp.dot(band[to], cells, preferred_element_type=F32)
    up_ref[...] = ud[...].reshape(2 * CELLS, HALF).T
    chip_rows(u_own, u_part, u_rows, row_sems, wait_copy)


def fill_outer(x, passed0, passed1, joined0, joined1, pole_ref):
    lat = my_lat()
    low, high = slice(0, WIN - EDGE), slice(CHIP - WIN + EDGE, CHIP)
    for side, (rows, joined, pole) in enumerate(((passed0, joined0, 0), (passed1, joined1, LAT - 1))):
        block, at, none = (HALO, 0, slice(2 * EDGE, WIN)) if side == 0 else (0, WIN - 2 * EDGE, slice(0, WIN - 2 * EDGE))
        for w, edges in enumerate((joined1, joined0)):
            x[side, w, block, none, :] = jnp.zeros((WIN - 2 * EDGE, CHANNELS), BF)
            x[side, w, block, at : at + 2 * EDGE, :] = edges[0 : 2 * EDGE]
            to = slice(EDGE, WIN) if w == 0 else slice(0, WIN - EDGE)
            for m in range(HALO):
                x[side, w, side + m, to, :] = rows[m, low if w == 0 else high]
        corners = joined.at[COLS : COLS + 2 * EDGE]

        @pl.when(lat != pole)
        def _():
            for w in range(2):
                at = w * (WIN - EDGE)
                for m in range(HALO):
                    x[side, w, side + m, at : at + EDGE, :] = spread_columns(corners, 0, m + (HALO if w == 0 else 0), w == 1)

        @pl.when(lat == pole)
        def _():
            for w in range(2):
                at = w * (WIN - EDGE)
                for m in range(HALO):
                    x[side, w, side + m, at : at + EDGE, :] = pole_ref[w, m]


def grad_kernel(p_own, p_part, j_own, j_part, pole_ref, acc, band, up, g_ref, own_ref, x, basis, g, sems):
    core = my_core()

    @pl.when(core == 0)
    def _():
        fill_outer(x, p_own, p_part, j_own, j_part, pole_ref)

    @pl.when(core == 1)
    def _():
        fill_outer(x, p_part, p_own, j_part, j_own, pole_ref)

    for i in range(ROWS):
        to = slice(i * NBASIS * COLS, (i + 1) * NBASIS * COLS)
        first, size = outer_rows(i)
        for w in range(2):
            cells = x[i // HALO, w].reshape(OUTER, CHANNELS)[first : first + size]
            rows = (acc[w, to] + jnp.dot(band[w, to, :size], cells, preferred_element_type=F32)).astype(BF)
            at = w * CELLS + i * COLS
            for k in range(NBASIS):
                basis[k, at : at + COLS, :] = rows[k * COLS : (k + 1) * COLS]
    at = pl.multiple_of(core * CELLS, CELLS)
    own_copy = pltpu.make_async_copy(basis.at[:, pl.ds(at, CELLS)], own_ref, sems.at[4])
    own_copy.start()
    outs = []
    for k in range(NBASIS):
        to = slice(k * CHANNELS, (k + 1) * CHANNELS)
        g[to, :] = jnp.dot(up[...], basis[k], preferred_element_type=F32).astype(BF).T
        outs.append(pltpu.make_async_copy(g.at[to], g_ref.at[to], sems.at[k]))
        outs[-1].start()
    own_copy.wait()
    each(outs, wait_copy)


def tie_kernel(rows, after, out):
    del rows, after, out


def conv_kernel(own_ref, w_ref, conv_ref):
    total = jnp.zeros((CELLS, CHANNELS), F32)
    for k in range(NBASIS):
        total = total + jnp.dot(own_ref[k], w_ref[k * CHANNELS : (k + 1) * CHANNELS, :], preferred_element_type=F32)
    conv_ref[...] = total.astype(BF).reshape(ROWS, COLS, CHANNELS)


def state_kernel(w_ref, vec_ref, u_own, u_part, p_own, p_part, a_own, a_part, state_ref, x, rim, bg, acc, sems):
    def inputs(act):
        fill(act, x, rim, sems, 1, (u_own, u_part), (p_own, p_part), (a_own, a_part))

    inputs(start_copy)
    inputs(wait_copy)

    @pl.when(my_core() == 0)
    def _():
        fill_rim(x, rim, 1, 0, None)

    @pl.when(my_core() == 1)
    def _():
        fill_rim(x, rim, 1, None, WIN - EDGE)

    for k in range(NBASIS):
        wk = w_ref[k * CHANNELS : (k + 1) * CHANNELS, :]
        for part in range(3):
            cells = x[part * 4 : (part + 1) * 4].reshape(4 * WIN, CHANNELS)
            got = lax.dot_general(cells, wk, (((1,), (1,)), ((), ())), preferred_element_type=F32)
            bg[part * 4 : (part + 1) * 4, k * WIN : (k + 1) * WIN, :] = got.astype(BF).reshape(4, WIN, CHANNELS)
    acc[...] = jnp.zeros((ROWS, COLS, CHANNELS), F32)
    for e in range(EXT):
        rows = [r for r in range(ROWS) if 0 <= r + TAPS - 1 - e < TAPS]
        blocks = []
        for r in rows:
            a = r + TAPS - 1 - e
            row = jnp.broadcast_to(vec_ref[a, e : e + 1, :], (COLS, SPAN))
            blocks.append(pltpu.roll(row, 0, 1, stride=1, stride_axis=0).astype(BF))
        got = jnp.dot(jnp.concatenate(blocks, 0), bg[e], preferred_element_type=F32)
        for n, r in enumerate(rows):
            acc[r] += got[n * COLS : (n + 1) * COLS]
    state_ref[...] = acc[...].astype(BF)


def total_kernel(pieces, out):
    for t in range(2):
        out[:, t * HALF : (t + 1) * HALF] = jnp.sum(pieces[:, t].astype(F32), 0)


def on_device(features, upstream, weights, filter_basis, lat_width, lat_offset, lon_reach):
    core = my_core()
    info = jnp.concatenate([lat_width, lat_offset, lon_reach])

    f_part = send(features, to_partner)
    u_part = send(upstream, to_partner)
    own_rows = jnp.where(core == 0, features[ROWS - HALO :], features[:HALO])
    rows = pl.pallas_call(
        rows_kernel,
        out_shape=jax.ShapeDtypeStruct((HALO, CHIP, CHANNELS), BF),
        in_specs=[ANY, ANY],
        out_specs=ANY,
        scratch_shapes=[pltpu.SemaphoreType.DMA((2 * HALO,))],
        compiler_params=params(4),
        cost_estimate=cost(1000, 2_000_000),
        name="rows",
    )(own_rows, f_part)
    af_own = send(rows, along_meridian)
    filt = jnp.transpose(filter_basis, (2, 3, 0, 1)).reshape(PLACES, NLAT)
    inner_band, outer_band = pl.pallas_call(
        bands_kernel,
        out_shape=(
            jax.ShapeDtypeStruct((TALL, BAND), BF),
            jax.ShapeDtypeStruct((2, TALL, OUTER), BF),
        ),
        in_specs=[SMEM, VMEM],
        out_specs=(VMEM, VMEM),
        compiler_params=params(16),
        cost_estimate=cost(2_000_000_000, 5_000_000),
        name="bands",
    )(info, filt)

    edges, corners = pl.pallas_call(
        edges_kernel,
        out_shape=(
            jax.ShapeDtypeStruct((PACKED, CHANNELS), BF),
            jax.ShapeDtypeStruct((PACKED, CHANNELS), BF),
        ),
        in_specs=[ANY] * 4,
        out_specs=(VMEM, VMEM),
        scratch_shapes=[
            pltpu.VMEM((2, ROWS, EDGE, CHANNELS), BF),
            pltpu.VMEM((2, 2, HALO, EDGE, CHANNELS), BF),
            pltpu.SemaphoreType.DMA((6,)),
        ],
        compiler_params=params(4),
        cost_estimate=cost(1000, 1_000_000),
        name="edges",
    )(features, f_part, upstream, u_part)
    e_own = send(edges, to_chip)
    c_own = send(corners, across)
    acc, up, pole, u_rows = pl.pallas_call(
        inner_kernel,
        out_shape=(
            jax.ShapeDtypeStruct((2, TALL, CHANNELS), F32),
            jax.ShapeDtypeStruct((HALF, 2 * CELLS), BF),
            jax.ShapeDtypeStruct((2, HALO, EDGE, CHANNELS), BF),
            jax.ShapeDtypeStruct((HALO, CHIP, CHANNELS), BF),
        ),
        in_specs=[ANY] * 4 + [VMEM],
        out_specs=(VMEM, VMEM, VMEM, ANY),
        scratch_shapes=[
            pltpu.VMEM((ROWS + 2, WIDE, CHANNELS), BF),
            pltpu.VMEM((2 * ROWS, COLS, HALF), BF),
            pltpu.SemaphoreType.DMA((4,)),
            pltpu.SemaphoreType.DMA((2 * HALO,)),
        ],
        compiler_params=params(28),
        cost_estimate=cost(4_000_000_000, 16_000_000),
        name="inner",
    )(features, f_part, upstream, u_part, inner_band)
    joined = pl.pallas_call(
        join_kernel,
        out_shape=jax.ShapeDtypeStruct((COLS + PACKED, CHANNELS), BF),
        in_specs=[VMEM, VMEM, ANY],
        out_specs=VMEM,
        compiler_params=params(4),
        cost_estimate=cost(1000, 300_000),
        name="join",
    )(e_own, c_own, up)
    j_part = send(joined, to_partner)
    passed, u_rows = pl.pallas_call(
        relay_kernel,
        out_shape=(
            jax.ShapeDtypeStruct((HALO, CHIP, CHANNELS), BF),
            jax.ShapeDtypeStruct((HALO, CHIP, CHANNELS), BF),
        ),
        in_specs=[VMEM, ANY, ANY],
        out_specs=(VMEM, ANY),
        input_output_aliases={1: 1},
        compiler_params=params(8),
        cost_estimate=cost(1000, 4_000_000),
        name="relay",
    )(af_own, u_rows, joined)
    p_part = send(passed, to_partner)
    au_own = send(u_rows, along_meridian)
    partial, basis_own = pl.pallas_call(
        grad_kernel,
        out_shape=(
            pltpu.HBM((NBASIS * CHANNELS, HALF), BF),
            pltpu.HBM((NBASIS, CELLS, CHANNELS), BF),
        ),
        in_specs=[VMEM] * 8,
        out_specs=(HBM, HBM),
        scratch_shapes=[
            pltpu.VMEM((2, 2, 1 + HALO, WIN, CHANNELS), BF),
            pltpu.VMEM((NBASIS, 2 * CELLS, CHANNELS), BF),
            pltpu.VMEM((NBASIS * CHANNELS, HALF), BF),
            pltpu.SemaphoreType.DMA((5,)),
        ],
        compiler_params=params(30),
        cost_estimate=cost(6_000_000_000, 12_000_000),
        name="grad",
    )(passed, p_part, joined, j_part, pole, acc, outer_band, up)

    pieces = lax.all_to_all(partial.reshape(LAT * LON, OWNED, HALF), BOTH, 0, 0, tiled=True)

    convolved = pl.pallas_call(
        conv_kernel,
        out_shape=jax.ShapeDtypeStruct((ROWS, COLS, CHANNELS), BF),
        in_specs=[VMEM] * 2,
        out_specs=VMEM,
        compiler_params=params(20),
        cost_estimate=cost(80_000_000_000, 8_000_000),
        name="conv",
    )(basis_own, weights)
    au_own = pl.pallas_call(
        tie_kernel,
        out_shape=jax.ShapeDtypeStruct(au_own.shape, BF),
        in_specs=[ANY, ANY],
        out_specs=ANY,
        input_output_aliases={0: 0},
        compiler_params=params(1),
        name="tie",
    )(au_own, in_hbm(convolved))
    au_part = send(au_own, to_partner)
    vecs = pl.pallas_call(
        spread_kernel,
        out_shape=jax.ShapeDtypeStruct((TAPS, 16, SPAN), F32),
        in_specs=[SMEM, VMEM, HBM],
        out_specs=VMEM,
        compiler_params=params(8),
        cost_estimate=cost(1_000_000_000, 1_000_000),
        name="spread",
    )(info, filt, in_hbm(convolved))
    state_grad = pl.pallas_call(
        state_kernel,
        out_shape=jax.ShapeDtypeStruct((ROWS, COLS, CHANNELS), BF),
        in_specs=[VMEM] * 2 + [ANY] * 6,
        out_specs=VMEM,
        scratch_shapes=[
            pltpu.VMEM((EXT, WIN, CHANNELS), BF),
            pltpu.VMEM((4, 2 * EDGE, CHANNELS), BF),
            pltpu.VMEM((EXT, SPAN, CHANNELS), BF),
            pltpu.VMEM((ROWS, COLS, CHANNELS), F32),
            pltpu.SemaphoreType.DMA((FILL_SEMS,)),
        ],
        compiler_params=params(28),
        cost_estimate=cost(8_000_000_000, 12_000_000),
        name="state",
    )(weights, vecs, upstream, u_part, joined, j_part, au_own, au_part)

    weight_grad = pl.pallas_call(
        total_kernel,
        out_shape=jax.ShapeDtypeStruct((OWNED, CHANNELS), F32),
        in_specs=[VMEM],
        out_specs=VMEM,
        compiler_params=params(16),
        name="total",
    )(pltpu.with_memory_space_constraint(pieces.reshape(LAT * LON // 2, 2, OWNED, HALF), pltpu.VMEM))
    return convolved, state_grad, weight_grad


def solution(mesh):
    return jax.shard_map(
        on_device,
        mesh=mesh,
        in_specs=(P("lat", "lon", None), P("lat", "lon", None), P(), P(), P(), P(), P()),
        out_specs=(P("lat", "lon", None), P("lat", "lon", None), P(("lat", "lon"), None)),
        check_vma=False,
    )
```
